512 devices in a mesh: blk: 64 (over z_hi, y, x), grid: 8 (over z_lo, core).
Axes of the slice: x: 4, y: 4, z: 16 (z_hi: 4, z_lo: 4; z = z_hi * 4 + z_lo), core: 2. Of those that a mesh axis runs over, the one named last changes fastest.
Arguments:
- bands: float32 [128, 96, 9216], P('blk', 'grid'), may hold values from -6 to 6
Outputs:
- exchange_field: float32 [128, 96, 9216], P('blk', 'grid')
The draws below stay inside these ranges and needn't reach their ends.
All inputs are finite; a program needn't handle non-finite values.
Results may differ from the reference program's by a relative error of at most 0.0003.
Values sent between devices are 32-bit elements; how exact they have to be, the bound alone decides.
A program may use at most 64 MiB of HBM per device.

```python
import jax
import jax.numpy as jnp
from jax import lax

NG = 96
B_DEV = 2
BANDS = 128


def draw_bands(key, part):
    key = jax.random.fold_in(key, 11)
    noise = jax.random.normal(key, (BANDS, NG, NG * NG), jnp.float32)
    return jnp.clip(noise, -6.0, 6.0)


def setup_inputs(seed: int = 0) -> dict:
    arg_keys = jax.random.split(jax.random.key(seed), 2)
    return {
        "bands": draw_bands(jax.random.fold_in(arg_keys[1], 71), 0),
    }


box_edge = 23.47


def coulomb_table():
    index = jnp.arange(NG, dtype=jnp.int32)
    folded = jnp.minimum(index, NG - index)
    square = folded * folded
    total = square[:, None, None] + square[None, :, None] + square[None, None, :]
    factor = 4.0 * jnp.pi / (2.0 * jnp.pi / box_edge) ** 2
    safe = jnp.maximum(total, 1).astype(jnp.float32)
    return jnp.where(total > 0, factor / safe, 0.0).astype(jnp.float32)


def solve_pair(density, coulomb):
    spectrum = jnp.fft.fftn(density)
    return jnp.real(jnp.fft.ifftn(spectrum * coulomb)).astype(jnp.float32)


def reference(bands):
    coulomb = coulomb_table()
    blocks = bands.reshape(BANDS // B_DEV, B_DEV, NG, NG, NG)
    behind = jnp.roll(blocks, 1, axis=0)

    def one_block(pair):
        own, before = pair
        own_terms = [jnp.zeros((NG, NG, NG), jnp.float32) for first in range(B_DEV)]
        back_terms = [jnp.zeros((NG, NG, NG), jnp.float32) for first in range(B_DEV)]
        for first in range(B_DEV):
            for second in range(first, B_DEV):
                field = solve_pair(own[first] * own[second], coulomb)
                own_terms[first] = own_terms[first] + field * own[second]
                if second != first:
                    own_terms[second] = own_terms[second] + field * own[first]
        for first in range(B_DEV):
            for second in range(B_DEV):
                field = solve_pair(own[first] * before[second], coulomb)
                own_terms[first] = own_terms[first] + field * before[second]
                back_terms[second] = back_terms[second] + field * own[first]
        return jnp.stack(own_terms), jnp.stack(back_terms)

    own_part, back_part = lax.map(one_block, (blocks, behind))
    total = own_part + jnp.roll(back_part, -1, axis=0)
    return (-total).reshape(BANDS, NG, NG * NG)
```

```python
import functools

import jax
import jax.numpy as jnp
import ml_dtypes
import numpy as np
from jax import lax
from jax.experimental import pallas as pl
from jax.experimental.pallas import tpu as pltpu
from jax.sharding import PartitionSpec as P

NG = 96
BOX_EDGE = 23.47
MESH = pl.DeviceIdType.MESH
F32 = jnp.float32
BF16 = jnp.bfloat16

GRID = 8
SLAB = NG // GRID
ROWS = NG * NG // 128
TILES = ROWS // GRID
MSG = 112
FIELDS = 7
LAG_SOLVE = 2
LAG_BACK = 5


def hartley(rows, cols):
    angle = (rows[:, None] * cols[None, :] % NG) * (2.0 * np.pi / NG)
    return np.cos(angle) + np.sin(angle)


def split_table(table):
    high = table.astype(np.float32).astype(ml_dtypes.bfloat16)
    low = (table - high.astype(np.float64)).astype(np.float32).astype(ml_dtypes.bfloat16)
    return high, low


def left_table(table):
    high, low = split_table(table)
    top = np.concatenate([high, high], axis=1)
    bottom = np.concatenate([low, np.zeros_like(low)], axis=1)
    return np.concatenate([top, bottom], axis=0)


def tables():
    plain = np.arange(NG)
    mixed = np.arange(NG) % GRID * SLAB + np.arange(NG) // GRID
    right = np.stack(split_table(hartley(plain, plain)))
    return (
        right,
        left_table(hartley(plain, plain)),
        left_table(hartley(plain, mixed)),
        left_table(hartley(mixed, plain)),
    )


def split(value):
    high = value.astype(BF16)
    low = (value - high.astype(F32)).astype(BF16)
    return high, low


def dot(a, b):
    return jnp.dot(a, b, preferred_element_type=F32)


def from_left(table, value):
    high, low = split(value)
    both = dot(table, jnp.concatenate([high, low], axis=0))
    return both[:NG] + both[NG:]


def from_right(value, right_ref):
    high, low = split(value)
    return dot(high, right_ref[0]) + (dot(low, right_ref[0]) + dot(high, right_ref[1]))


def pack(plane):
    last = plane[72:96]
    return [
        jnp.concatenate([plane[24 * k : 24 * k + 24], last[:, 32 * k : 32 * k + 32]], axis=1)
        for k in range(3)
    ]


def unpack(parts):
    last = jnp.concatenate([part[:, 96:128] for part in parts], axis=1)
    return jnp.concatenate([part[:, :96] for part in parts] + [last], axis=0)


def kernel(
    blocks,
    own_ref,
    right_ref,
    plane_ref,
    there_ref,
    back_ref,
    out_ref,
    bands,
    acc,
    coulomb,
    sent,
    got,
    ret_sent,
    ret_got,
    band_out,
    band_in,
    theirs_out,
    theirs_in,
    fwd_send,
    fwd_recv,
    bwd_send,
    bwd_recv,
    self_sem,
    blk_send,
    blk_recv,
):
    blk = lax.axis_index("blk")
    me = lax.axis_index("grid")
    after = lax.rem(blk + 1, blocks)
    before = lax.rem(blk + blocks - 1, blocks)

    barrier = pltpu.get_barrier_semaphore()
    for d in range(1, GRID):
        pl.semaphore_signal(
            barrier, inc=1, device_id=(blk, lax.rem(me + d, GRID)), device_id_type=MESH
        )
    for other in (after, before):
        pl.semaphore_signal(barrier, inc=1, device_id=(other, me), device_id_type=MESH)
    pl.semaphore_wait(barrier, GRID + 1)

    def message(field, device):
        return pl.ds(pl.multiple_of((field * GRID + device) * MSG, 8), MSG)

    def exchange(source, target, send_sem, recv_sem, field, peer):
        return pltpu.make_async_remote_copy(
            src_ref=source.at[message(field, peer)],
            dst_ref=target.at[message(field, me)],
            send_sem=send_sem.at[field, peer],
            recv_sem=recv_sem.at[field, me],
            device_id=(blk, peer),
            device_id_type=MESH,
        )

    def arrival(source, target, send_sem, recv_sem, field, peer):
        return pltpu.make_async_remote_copy(
            src_ref=source.at[message(field, peer)],
            dst_ref=target.at[message(field, peer)],
            send_sem=send_sem.at[field, peer],
            recv_sem=recv_sem.at[field, peer],
            device_id=(blk, peer),
            device_id_type=MESH,
        )

    def keep(source, target, field, way):
        here = message(field, me)
        return pltpu.make_async_copy(source.at[here], target.at[here], self_sem.at[way, field])

    def send_all(source, target, send_sem, recv_sem, field, way):
        for d in (4, 3, 5, 2, 6, 1, 7):
            exchange(source, target, send_sem, recv_sem, field, lax.rem(me + d, GRID)).start()
        keep(source, target, field, way).start()

    def await_all(source, target, send_sem, recv_sem, field, way):
        keep(source, target, field, way).wait()
        for d in range(1, GRID):
            peer = lax.rem(me + d, GRID)
            arrival(source, target, send_sem, recv_sem, field, peer).wait_recv()

    def band_rows(band):
        return pl.ds(pl.multiple_of(band * (SLAB * ROWS), 8), SLAB * ROWS)

    def to_block(source, target, way, band, other):
        return pltpu.make_async_remote_copy(
            src_ref=source.at[band_rows(band)],
            dst_ref=target.at[band_rows(band)],
            send_sem=blk_send.at[way, band],
            recv_sem=blk_recv.at[way, band],
            device_id=(other, me),
            device_id_type=MESH,
        )

    def put_packed(ref, band, x, plane):
        start = pl.multiple_of((band * SLAB + x) * ROWS, 8)
        for k, part in enumerate(pack(plane)):
            ref[pl.ds(start + 24 * k, 24), :] = part

    def get_packed(ref, band, x):
        start = pl.multiple_of((band * SLAB + x) * ROWS, 8)
        return unpack([ref[pl.ds(start + 24 * k, 24), :] for k in range(3)])

    for band in range(2):

        @pl.loop(0, SLAB)
        def _(x):
            plane = own_ref[band, x]
            bands[band, x] = plane
            put_packed(band_out, band, x, plane)

        to_block(band_out, band_in, 0, band, after).start()

    acc[...] = jnp.zeros_like(acc)

    def pair(field):
        first = jnp.where(field < 3, field // 2, (field + 1) % 2)
        second = jnp.where(field < 3, (field + 1) // 2, 2 + (field - 3) // 2)
        return first, second

    def forward(field):
        first, second = pair(field)
        for group in range(0, SLAB, 4):
            density = bands[first, pl.ds(group, 4)] * bands[second, pl.ds(group, 4)]
            along_z = from_right(density.reshape(4 * NG, NG), right_ref)
            for i in range(4):
                plane = from_left(plane_ref[...], along_z[i * NG : (i + 1) * NG])
                parts = pack(plane)
                for t in range(TILES):
                    tile = parts[t // 3][t % 3 * 8 : t % 3 * 8 + 8]
                    sent[
                        pl.ds(field * (GRID * MSG) + t * SLAB + group + i, GRID, stride=MSG), :
                    ] = tile
        send_all(sent, got, fwd_send, fwd_recv, field, 0)

    def make_coulomb():
        factor = 4.0 * np.pi / (2.0 * np.pi / BOX_EDGE) ** 2 / float(NG) ** 3

        def square(index):
            folded = jnp.minimum(index, NG - index)
            return folded * folded

        kx = lax.broadcasted_iota(jnp.int32, (NG, 128), 0)
        lane = lax.broadcasted_iota(jnp.int32, (NG, 128), 1)

        @pl.loop(0, TILES)
        def _(t):
            row = t * GRID + me
            part, a = row // 24, row % 24
            ky = jnp.where(lane < NG, 24 * part + a, 72 + a)
            kz = jnp.where(lane < NG, lane, 32 * part + lane - NG)
            total = square(kx) + square(ky) + square(kz)
            safe = jnp.maximum(total, 1).astype(F32)
            coulomb[t] = jnp.where(total > 0, factor / safe, 0.0)

    def solve(field):
        await_all(sent, got, fwd_send, fwd_recv, field, 0)
        base = field * (GRID * MSG)
        for t in range(TILES):
            column = jnp.concatenate(
                [
                    got[pl.ds(base + t * SLAB + x, GRID, stride=MSG), :]
                    for x in range(SLAB)
                ],
                axis=0,
            )
            spectrum = from_left(there_ref[...], column) * coulomb[t]
            mixed = from_left(back_ref[...], spectrum)
            for x in range(SLAB):
                ret_sent[pl.ds(base + t * SLAB + x, GRID, stride=MSG), :] = mixed[
                    x * GRID : (x + 1) * GRID
                ]
        send_all(ret_sent, ret_got, bwd_send, bwd_recv, field, 1)

    def backward(field):
        await_all(ret_sent, ret_got, bwd_send, bwd_recv, field, 1)
        first, second = pair(field)
        base = field * (GRID * MSG)
        for group in range(0, SLAB, 4):
            planes = []
            for i in range(4):
                tiles = [
                    ret_got[pl.ds(base + t * SLAB + group + i, GRID, stride=MSG), :]
                    for t in range(TILES)
                ]
                parts = [jnp.concatenate(tiles[3 * k : 3 * k + 3], axis=0) for k in range(3)]
                planes.append(from_left(plane_ref[...], unpack(parts)))
            potential = from_right(jnp.concatenate(planes, axis=0), right_ref)
            potential = potential.reshape(4, NG, NG)
            here = pl.ds(group, 4)
            acc[first, here] += potential * bands[second, here]

            @pl.when(first != second)
            def _():
                acc[second, here] += potential * bands[first, here]

    def give_back(band):
        @pl.loop(0, SLAB)
        def _(x):
            put_packed(theirs_out, band, x, acc[2 + band, x])

        to_block(theirs_out, theirs_in, 1, band, before).start()

    @pl.loop(0, FIELDS + LAG_BACK)
    def _(step):
        @pl.when(step == 3)
        def _():
            for band in range(2):
                to_block(band_out, band_in, 0, band, after).wait_recv()

                @pl.loop(0, SLAB)
                def _(x):
                    bands[2 + band, x] = get_packed(band_in, band, x)

        @pl.when(step < FIELDS)
        def _():
            forward(step)

        @pl.when(step == 1)
        def _():
            make_coulomb()

        @pl.when((step >= LAG_SOLVE) & (step < FIELDS + LAG_SOLVE))
        def _():
            solve(step - LAG_SOLVE)

        @pl.when(step >= LAG_BACK)
        def _():
            backward(step - LAG_BACK)

        @pl.when(step == LAG_BACK + 4)
        def _():
            give_back(0)

    give_back(1)

    for band in range(2):
        to_block(theirs_out, theirs_in, 1, band, before).wait_recv()

        @pl.loop(0, SLAB)
        def _(x):
            out_ref[band, x] = -(acc[band, x] + get_packed(theirs_in, band, x))

    @pl.loop(0, FIELDS)
    def _(field):
        for d in range(1, GRID):
            peer = lax.rem(me + d, GRID)
            exchange(sent, got, fwd_send, fwd_recv, field, peer).wait_send()
            exchange(ret_sent, ret_got, bwd_send, bwd_recv, field, peer).wait_send()

    for band in range(2):
        to_block(band_out, band_in, 0, band, after).wait_send()
        to_block(theirs_out, theirs_in, 1, band, before).wait_send()


def body(blocks, bands):
    count, slab, plane = bands.shape
    own = bands.reshape(count, slab, NG, NG)
    constants = [jnp.asarray(table) for table in tables()]
    vmem = pl.BlockSpec(memory_space=pltpu.VMEM)
    messages = pltpu.VMEM((FIELDS * GRID * MSG, 128), F32)
    packed = pltpu.VMEM((count * SLAB * ROWS, 128), F32)
    out = pl.pallas_call(
        functools.partial(kernel, blocks),
        out_shape=jax.ShapeDtypeStruct((count, slab, NG, NG), F32),
        in_specs=[vmem] * 5,
        out_specs=vmem,
        scratch_shapes=[
            pltpu.VMEM((2 * count, SLAB, NG, NG), F32),
            pltpu.VMEM((2 * count, SLAB, NG, NG), F32),
            pltpu.VMEM((TILES, NG, 128), F32),
            messages,
            messages,
            messages,
            messages,
            packed,
            packed,
            packed,
            packed,
            pltpu.SemaphoreType.DMA((FIELDS, GRID)),
            pltpu.SemaphoreType.DMA((FIELDS, GRID)),
            pltpu.SemaphoreType.DMA((FIELDS, GRID)),
            pltpu.SemaphoreType.DMA((FIELDS, GRID)),
            pltpu.SemaphoreType.DMA((2, FIELDS)),
            pltpu.SemaphoreType.DMA((2, 2)),
            pltpu.SemaphoreType.DMA((2, 2)),
        ],
        compiler_params=pltpu.CompilerParams(
            collective_id=0, has_side_effects=True, vmem_limit_bytes=48 * 1024 * 1024
        ),
    )(own, *constants)
    return out.reshape(count, slab, plane)


def solution(mesh):
    spec = P("blk", "grid", None)
    return jax.shard_map(
        functools.partial(body, mesh.shape["blk"]),
        mesh=mesh,
        in_specs=(spec,),
        out_specs=spec,
        check_vma=False,
    )
```

```python
import functools

import jax
import jax.numpy as jnp
import ml_dtypes
import numpy as np
from jax import lax
from jax.experimental import pallas as pl
from jax.experimental.pallas import tpu as pltpu
from jax.sharding import PartitionSpec as P

NG = 96
BOX_EDGE = 23.47
MESH = pl.DeviceIdType.MESH
F32 = jnp.float32
BF16 = jnp.bfloat16

GRID = 8
SLAB = NG // GRID
ROWS = NG * NG // 128
TILES = ROWS // GRID
MSG = 112
FIELDS = 7

LAYER = 16
COLUMNS = (0, 1, 2, 3, 4, 7, 8, 11, 12, 13, 14, 15)
BETWEEN = LAYER - 1, 0

FORWARD = (0, 1, 2, -1, 3, 4, 5, 6, -1, -1, -1, -1, -1, -1)
SOLVE = (-1, -1, 0, 1, -1, -1, 3, 4, 5, 6, 2, -1, -1, -1)
BACKWARD = (-1, -1, -1, -1, -1, -1, -1, 0, 1, 3, 4, 5, 6, 2)


def hartley(rows, cols):
    angle = (rows[:, None] * cols[None, :] % NG) * (2.0 * np.pi / NG)
    return np.cos(angle) + np.sin(angle)


def split_table(table):
    parts = []
    for _ in range(3):
        part = table.astype(np.float32).astype(ml_dtypes.bfloat16)
        parts.append(part)
        table = table - part.astype(np.float64)
    return parts


def left_table(table):
    return np.concatenate([np.concatenate([part, part], axis=1) for part in split_table(table)])


def right_table(table):
    parts = [np.pad(part, ((0, 0), (0, 128 - NG))) for part in split_table(table)]
    return np.concatenate(parts, axis=1)


def tables():
    plain = np.arange(NG)
    mixed = np.arange(NG) % GRID * SLAB + np.arange(NG) // GRID
    return (
        right_table(hartley(plain, plain)),
        left_table(hartley(plain, plain)),
        left_table(hartley(plain, mixed)),
        left_table(hartley(mixed, plain)),
    )


def split(value):
    high = value.astype(BF16)
    low = (value - high.astype(F32)).astype(BF16)
    return high, low


def dot(a, b):
    return jnp.dot(a, b, preferred_element_type=F32)


def from_left(table, value):
    high, low = split(value)
    both = dot(table, jnp.concatenate([high, low], axis=0))
    return both[:NG] + (both[NG : 2 * NG] + both[2 * NG :])


def from_right(value, right_ref):
    high, low = split(value)
    above = dot(high, right_ref[:, :256])
    below = dot(low, right_ref[:, :256])
    rest = dot(high, right_ref[:, 256:])
    second = above[:, 128 : 128 + NG] + below[:, :NG]
    return above[:, :NG] + (second + (below[:, 128 : 128 + NG] + rest[:, :NG]))


def pack(plane):
    last = plane[72:96]
    return [
        jnp.concatenate([plane[24 * k : 24 * k + 24], last[:, 32 * k : 32 * k + 32]], axis=1)
        for k in range(3)
    ]


def unpack(parts):
    last = jnp.concatenate([part[:, 96:128] for part in parts], axis=1)
    return jnp.concatenate([part[:, :96] for part in parts] + [last], axis=0)


def kernel(
    blocks,
    own_ref,
    right_ref,
    plane_ref,
    there_ref,
    back_ref,
    out_ref,
    bands,
    acc,
    coulomb,
    sent,
    got,
    ret_sent,
    ret_got,
    band_out,
    band_in,
    theirs_out,
    theirs_in,
    fwd_send,
    fwd_recv,
    bwd_send,
    bwd_recv,
    self_sem,
    blk_send,
    blk_recv,
    first_stop,
    second_stop,
    first_send,
    first_recv,
    second_send,
    second_recv,
    third_send,
    last_recv,
):
    blk = lax.axis_index("blk")
    me = lax.axis_index("grid")
    after = lax.rem(blk + 1, blocks)
    before = lax.rem(blk + blocks - 1, blocks)

    column = lax.rem(blk, LAYER)
    layer = blk - column
    piece = sum(jnp.where(column == c, i, 0) for i, c in enumerate(COLUMNS))
    relays = functools.reduce(jnp.logical_or, [column == c for c in COLUMNS])

    barrier = pltpu.get_barrier_semaphore()

    def greet(other):
        pl.semaphore_signal(barrier, inc=1, device_id=other, device_id_type=MESH)

    for d in range(1, GRID):
        greet((blk, lax.rem(me + d, GRID)))

    at_end = (column == 0) | (column == LAYER - 1)
    peers = GRID - 1 + jnp.where(relays, 2, 0)
    for c in range(LAYER):
        linked = (column == c - 1) | (column == c + 1)
        if c in COLUMNS:
            linked = linked | ((relays if c in BETWEEN else at_end) & (column != c))
        peers = peers + jnp.where(linked, 1, 0)

        @pl.when(linked)
        def _():
            greet((layer + c, me))

    @pl.when(relays)
    def _():
        greet((lax.rem(blk + LAYER, blocks), me))
        greet((lax.rem(blk + blocks - LAYER, blocks), me))

    pl.semaphore_wait(barrier, peers)

    def message(field, device):
        return pl.ds(pl.multiple_of((field * GRID + device) * MSG, 8), MSG)

    def exchange(source, target, send_sem, recv_sem, field, peer):
        return pltpu.make_async_remote_copy(
            src_ref=source.at[message(field, peer)],
            dst_ref=target.at[message(field, me)],
            send_sem=send_sem.at[field, peer],
            recv_sem=recv_sem.at[field, me],
            device_id=(blk, peer),
            device_id_type=MESH,
        )

    def arrival(source, target, send_sem, recv_sem, field, peer):
        return pltpu.make_async_remote_copy(
            src_ref=source.at[message(field, peer)],
            dst_ref=target.at[message(field, peer)],
            send_sem=send_sem.at[field, peer],
            recv_sem=recv_sem.at[field, peer],
            device_id=(blk, peer),
            device_id_type=MESH,
        )

    def keep(source, target, field, way):
        here = message(field, me)
        return pltpu.make_async_copy(source.at[here], target.at[here], self_sem.at[way, field])

    def send_all(source, target, send_sem, recv_sem, field, way):
        for d in (4, 3, 5, 2, 6, 1, 7):
            exchange(source, target, send_sem, recv_sem, field, lax.rem(me + d, GRID)).start()
        keep(source, target, field, way).start()

    def await_all(source, target, send_sem, recv_sem, field, way):
        keep(source, target, field, way).wait()
        for d in range(1, GRID):
            peer = lax.rem(me + d, GRID)
            arrival(source, target, send_sem, recv_sem, field, peer).wait_recv()

    def band_rows(band):
        return pl.ds(pl.multiple_of(band * (SLAB * ROWS), 8), SLAB * ROWS)

    travel = ((band_out, band_in), (theirs_out, theirs_in))
    planes = SLAB // len(COLUMNS)

    def piece_rows(band, index):
        return pl.ds(pl.multiple_of((band * SLAB + index * planes) * ROWS, 8), planes * ROWS)

    def stop_rows(way, band):
        return pl.ds((way * 2 + band) * planes * ROWS, planes * ROWS)

    def to_block(way, band):
        source, target = travel[way]
        return pltpu.make_async_remote_copy(
            src_ref=source.at[band_rows(band)],
            dst_ref=target.at[band_rows(band)],
            send_sem=blk_send.at[way, band],
            recv_sem=blk_recv.at[way, band],
            device_id=((after, before)[way], me),
            device_id_type=MESH,
        )

    def to_column(way, band, index):
        return pltpu.make_async_remote_copy(
            src_ref=travel[way][0].at[piece_rows(band, index)],
            dst_ref=first_stop.at[stop_rows(way, band)],
            send_sem=first_send.at[way, band, index],
            recv_sem=first_recv.at[way, band],
            device_id=(layer + COLUMNS[index], me),
            device_id_type=MESH,
        )

    def along_column(way, band, start, end):
        source = first_stop.at[stop_rows(way, band)]
        if start:
            source = travel[way][0].at[piece_rows(band, COLUMNS.index(BETWEEN[way]))]
        target, done = second_stop.at[stop_rows(way, band)], second_recv.at[way, band]
        if end:
            index = COLUMNS.index(BETWEEN[1 - way])
            target = travel[way][1].at[piece_rows(band, index)]
            done = last_recv.at[way, band, index]
        next_layer = lax.rem(blk + (LAYER if way == 0 else blocks - LAYER), blocks)
        return pltpu.make_async_remote_copy(
            src_ref=source,
            dst_ref=target,
            send_sem=second_send.at[way, band],
            recv_sem=done,
            device_id=(next_layer, me),
            device_id_type=MESH,
        )

    def from_column(way, band, index):
        return pltpu.make_async_remote_copy(
            src_ref=second_stop.at[stop_rows(way, band)],
            dst_ref=travel[way][1].at[piece_rows(band, index)],
            send_sem=third_send.at[way, band],
            recv_sem=last_recv.at[way, band, index],
            device_id=(layer + BETWEEN[1 - way], me),
            device_id_type=MESH,
        )

    def depart(way, band):
        start = BETWEEN[way]

        @pl.when(column != start)
        def _():
            to_block(way, band).start()

        @pl.when(column == start)
        def _():
            along_column(way, band, True, False).start()
            for index, c in enumerate(COLUMNS):
                if c != start:
                    to_column(way, band, index).start()

    def relay_along(way, band):
        start, end = BETWEEN[way], BETWEEN[1 - way]

        @pl.when(relays & (column != start))
        def _():
            to_column(way, band, 0).wait_recv()

            @pl.when(column == end)
            def _():
                along_column(way, band, False, True).start()

            @pl.when(column != end)
            def _():
                along_column(way, band, False, False).start()

    def relay_in(way, band):
        @pl.when(relays & (column != BETWEEN[1 - way]))
        def _():
            along_column(way, band, False, False).wait_recv()
            from_column(way, band, piece).start()

    def arrive(way, band):
        end = BETWEEN[1 - way]

        @pl.when(column != end)
        def _():
            to_block(way, band).wait_recv()

        @pl.when(column == end)
        def _():
            for index in range(len(COLUMNS)):
                from_column(way, band, index).wait_recv()

    def departed(way, band):
        start, end = BETWEEN[way], BETWEEN[1 - way]

        @pl.when(column != start)
        def _():
            to_block(way, band).wait_send()

        @pl.when(column == start)
        def _():
            for index, c in enumerate(COLUMNS):
                if c != start:
                    to_column(way, band, index).wait_send()

        @pl.when(relays)
        def _():
            along_column(way, band, False, False).wait_send()

        @pl.when(relays & (column != end))
        def _():
            from_column(way, band, 0).wait_send()

    def put_packed(ref, band, x, plane):
        start = pl.multiple_of((band * SLAB + x) * ROWS, 8)
        for k, part in enumerate(pack(plane)):
            ref[pl.ds(start + 24 * k, 24), :] = part

    def get_packed(ref, band, x):
        start = pl.multiple_of((band * SLAB + x) * ROWS, 8)
        return unpack([ref[pl.ds(start + 24 * k, 24), :] for k in range(3)])

    for band in range(2):

        @pl.loop(0, SLAB)
        def _(x):
            plane = own_ref[band, x]
            bands[band, x] = plane
            put_packed(band_out, band, x, plane)

        depart(0, band)

    acc[...] = jnp.zeros_like(acc)

    def pair(field):
        first = jnp.where(field < 3, field // 2, (field + 1) % 2)
        second = jnp.where(field < 3, (field + 1) // 2, 2 + (field - 3) // 2)
        return first, second

    def forward(field):
        first, second = pair(field)
        for group in range(0, SLAB, 4):
            density = bands[first, pl.ds(group, 4)] * bands[second, pl.ds(group, 4)]
            along_z = from_right(density.reshape(4 * NG, NG), right_ref)
            for i in range(4):
                plane = from_left(plane_ref[...], along_z[i * NG : (i + 1) * NG])
                parts = pack(plane)
                for t in range(TILES):
                    tile = parts[t // 3][t % 3 * 8 : t % 3 * 8 + 8]
                    sent[
                        pl.ds(field * (GRID * MSG) + t * SLAB + group + i, GRID, stride=MSG), :
                    ] = tile
        send_all(sent, got, fwd_send, fwd_recv, field, 0)

    def make_coulomb():
        factor = 4.0 * np.pi / (2.0 * np.pi / BOX_EDGE) ** 2 / float(NG) ** 3

        def square(index):
            folded = jnp.minimum(index, NG - index)
            return folded * folded

        kx = lax.broadcasted_iota(jnp.int32, (NG, 128), 0)
        lane = lax.broadcasted_iota(jnp.int32, (NG, 128), 1)

        @pl.loop(0, TILES)
        def _(t):
            row = t * GRID + me
            part, a = row // 24, row % 24
            ky = jnp.where(lane < NG, 24 * part + a, 72 + a)
            kz = jnp.where(lane < NG, lane, 32 * part + lane - NG)
            total = square(kx) + square(ky) + square(kz)
            safe = jnp.maximum(total, 1).astype(F32)
            coulomb[t] = jnp.where(total > 0, factor / safe, 0.0)

    def solve(field):
        await_all(sent, got, fwd_send, fwd_recv, field, 0)
        base = field * (GRID * MSG)
        for t in range(TILES):
            column = jnp.concatenate(
                [
                    got[pl.ds(base + t * SLAB + x, GRID, stride=MSG), :]
                    for x in range(SLAB)
                ],
                axis=0,
            )
            spectrum = from_left(there_ref[...], column) * coulomb[t]
            mixed = from_left(back_ref[...], spectrum)
            for x in range(SLAB):
                ret_sent[pl.ds(base + t * SLAB + x, GRID, stride=MSG), :] = mixed[
                    x * GRID : (x + 1) * GRID
                ]
        send_all(ret_sent, ret_got, bwd_send, bwd_recv, field, 1)

    def backward(field):
        await_all(ret_sent, ret_got, bwd_send, bwd_recv, field, 1)
        first, second = pair(field)
        base = field * (GRID * MSG)
        for group in range(0, SLAB, 4):
            planes = []
            for i in range(4):
                tiles = [
                    ret_got[pl.ds(base + t * SLAB + group + i, GRID, stride=MSG), :]
                    for t in range(TILES)
                ]
                parts = [jnp.concatenate(tiles[3 * k : 3 * k + 3], axis=0) for k in range(3)]
                planes.append(from_left(plane_ref[...], unpack(parts)))
            potential = from_right(jnp.concatenate(planes, axis=0), right_ref)
            potential = potential.reshape(4, NG, NG)
            here = pl.ds(group, 4)
            acc[first, here] += potential * bands[second, here]

            @pl.when(first != second)
            def _():
                acc[second, here] += potential * bands[first, here]

    def give_back(band):
        @pl.loop(0, SLAB)
        def _(x):
            put_packed(theirs_out, band, x, acc[2 + band, x])

        depart(1, band)

    def at(step, fields):
        return sum(jnp.where(step == i, field, 0) for i, field in enumerate(fields))

    @pl.loop(0, len(FORWARD))
    def _(step):
        @pl.when(step == 2)
        def _():
            for band in range(2):
                relay_along(0, band)

        @pl.when(step == 4)
        def _():
            for band in range(2):
                relay_in(0, band)
            for band in range(2):
                arrive(0, band)

                @pl.loop(0, SLAB)
                def _(x):
                    bands[2 + band, x] = get_packed(band_in, band, x)

        forward_field = at(step, FORWARD)

        @pl.when(forward_field >= 0)
        def _():
            forward(forward_field)

        @pl.when(step == 1)
        def _():
            make_coulomb()

        solve_field = at(step, SOLVE)

        @pl.when(solve_field >= 0)
        def _():
            solve(solve_field)

        @pl.when(step == 13)
        def _():
            relay_in(1, 0)
            relay_along(1, 1)

        backward_field = at(step, BACKWARD)

        @pl.when(backward_field >= 0)
        def _():
            backward(backward_field)

        @pl.when(step == 10)
        def _():
            give_back(0)

        @pl.when(step == 11)
        def _():
            relay_along(1, 0)

        @pl.when(step == 12)
        def _():
            give_back(1)

    relay_in(1, 1)

    for band in range(2):
        arrive(1, band)

        @pl.loop(0, SLAB)
        def _(x):
            out_ref[band, x] = -(acc[band, x] + get_packed(theirs_in, band, x))

    @pl.loop(0, FIELDS)
    def _(field):
        for d in range(1, GRID):
            peer = lax.rem(me + d, GRID)
            exchange(sent, got, fwd_send, fwd_recv, field, peer).wait_send()
            exchange(ret_sent, ret_got, bwd_send, bwd_recv, field, peer).wait_send()

    for band in range(2):
        for way in range(2):
            departed(way, band)


def body(blocks, bands):
    count, slab, plane = bands.shape
    own = bands.reshape(count, slab, NG, NG)
    constants = [jnp.asarray(table) for table in tables()]
    vmem = pl.BlockSpec(memory_space=pltpu.VMEM)
    messages = pltpu.VMEM((FIELDS * GRID * MSG, 128), F32)
    packed = pltpu.VMEM((count * SLAB * ROWS, 128), F32)
    stops = pltpu.VMEM((2 * count * (SLAB // len(COLUMNS)) * ROWS, 128), F32)
    out = pl.pallas_call(
        functools.partial(kernel, blocks),
        out_shape=jax.ShapeDtypeStruct((count, slab, NG, NG), F32),
        in_specs=[vmem] * 5,
        out_specs=vmem,
        scratch_shapes=[
            pltpu.VMEM((2 * count, SLAB, NG, NG), F32),
            pltpu.VMEM((2 * count, SLAB, NG, NG), F32),
            pltpu.VMEM((TILES, NG, 128), F32),
            messages,
            messages,
            messages,
            messages,
            packed,
            packed,
            packed,
            packed,
            pltpu.SemaphoreType.DMA((FIELDS, GRID)),
            pltpu.SemaphoreType.DMA((FIELDS, GRID)),
            pltpu.SemaphoreType.DMA((FIELDS, GRID)),
            pltpu.SemaphoreType.DMA((FIELDS, GRID)),
            pltpu.SemaphoreType.DMA((2, FIELDS)),
            pltpu.SemaphoreType.DMA((2, 2)),
            pltpu.SemaphoreType.DMA((2, 2)),
            stops,
            stops,
            pltpu.SemaphoreType.DMA((2, 2, len(COLUMNS))),
            pltpu.SemaphoreType.DMA((2, 2)),
            pltpu.SemaphoreType.DMA((2, 2)),
            pltpu.SemaphoreType.DMA((2, 2)),
            pltpu.SemaphoreType.DMA((2, 2)),
            pltpu.SemaphoreType.DMA((2, 2, len(COLUMNS))),
        ],
        compiler_params=pltpu.CompilerParams(
            collective_id=0, has_side_effects=True, vmem_limit_bytes=48 * 1024 * 1024
        ),
    )(own, *constants)
    return out.reshape(count, slab, plane)


def solution(mesh):
    spec = P("blk", "grid", None)
    return jax.shard_map(
        functools.partial(body, mesh.shape["blk"]),
        mesh=mesh,
        in_specs=(spec,),
        out_specs=spec,
        check_vma=False,
    )
```

```python
import functools

import jax
import jax.numpy as jnp
import ml_dtypes
import numpy as np
from jax import lax
from jax.experimental import pallas as pl
from jax.experimental.pallas import tpu as pltpu
from jax.sharding import PartitionSpec as P

NG = 96
BOX_EDGE = 23.47
MESH = pl.DeviceIdType.MESH
F32 = jnp.float32
BF16 = jnp.bfloat16

GRID = 8
SLAB = NG // GRID
ROWS = NG * NG // 128
TILES = ROWS // GRID
MSG = 112
FIELDS = 7

LAYER = 16
COLUMNS = (0, 1, 2, 3, 4, 7, 8, 11, 12, 13, 14, 15)
BETWEEN = LAYER - 1, 0

FORWARD = (0, 1, 2, 3, 4, 5, 6, -1, -1, -1, -1, -1, -1, -1, -1)
SOLVE = (-1, -1, 0, -1, -1, -1, 3, 4, 5, 6, 1, 2, -1, -1, -1)
BACKWARD = (-1, -1, -1, -1, -1, -1, 0, -1, -1, 3, 4, 5, 6, 1, 2)


def hartley(rows, cols):
    angle = (rows[:, None] * cols[None, :] % NG) * (2.0 * np.pi / NG)
    return np.cos(angle) + np.sin(angle)


def split_table(table):
    parts = []
    for _ in range(3):
        part = table.astype(np.float32).astype(ml_dtypes.bfloat16)
        parts.append(part)
        table = table - part.astype(np.float64)
    return parts


def left_table(table):
    return np.concatenate([np.concatenate([part, part], axis=1) for part in split_table(table)])


def right_table(table):
    parts = [np.pad(part, ((0, 0), (0, 128 - NG))) for part in split_table(table)]
    return np.concatenate(parts, axis=1)


def tables():
    plain = np.arange(NG)
    mixed = np.arange(NG) % GRID * SLAB + np.arange(NG) // GRID
    return (
        right_table(hartley(plain, plain)),
        left_table(hartley(plain, plain)),
        left_table(hartley(plain, mixed)),
        left_table(hartley(mixed, plain)),
    )


def split(value):
    high = value.astype(BF16)
    low = (value - high.astype(F32)).astype(BF16)
    return high, low


def dot(a, b):
    return jnp.dot(a, b, preferred_element_type=F32)


def from_left(table, value):
    high, low = split(value)
    both = dot(table, jnp.concatenate([high, low], axis=0))
    return both[:NG] + (both[NG : 2 * NG] + both[2 * NG :])


def from_right(value, right_ref):
    high, low = split(value)
    above = dot(high, right_ref[:, :256])
    below = dot(low, right_ref[:, :256])
    rest = dot(high, right_ref[:, 256:])
    second = above[:, 128 : 128 + NG] + below[:, :NG]
    return above[:, :NG] + (second + (below[:, 128 : 128 + NG] + rest[:, :NG]))


def pack(plane):
    last = plane[72:96]
    return [
        jnp.concatenate([plane[24 * k : 24 * k + 24], last[:, 32 * k : 32 * k + 32]], axis=1)
        for k in range(3)
    ]


def unpack(parts):
    last = jnp.concatenate([part[:, 96:128] for part in parts], axis=1)
    return jnp.concatenate([part[:, :96] for part in parts] + [last], axis=0)


def kernel(
    blocks,
    own_ref,
    right_ref,
    plane_ref,
    there_ref,
    back_ref,
    out_ref,
    bands,
    acc,
    coulomb,
    sent,
    got,
    ret_sent,
    ret_got,
    band_out,
    band_in,
    theirs_out,
    theirs_in,
    fwd_send,
    fwd_recv,
    bwd_send,
    bwd_recv,
    self_sem,
    blk_send,
    blk_recv,
    first_stop,
    second_stop,
    first_send,
    first_recv,
    second_send,
    second_recv,
    third_send,
    last_recv,
):
    blk = lax.axis_index("blk")
    me = lax.axis_index("grid")
    after = lax.rem(blk + 1, blocks)
    before = lax.rem(blk + blocks - 1, blocks)

    column = lax.rem(blk, LAYER)
    layer = blk - column
    piece = sum(jnp.where(column == c, i, 0) for i, c in enumerate(COLUMNS))
    relays = functools.reduce(jnp.logical_or, [column == c for c in COLUMNS])

    barrier = pltpu.get_barrier_semaphore()

    def greet(other):
        pl.semaphore_signal(barrier, inc=1, device_id=other, device_id_type=MESH)

    for d in range(1, GRID):
        greet((blk, lax.rem(me + d, GRID)))

    at_end = (column == 0) | (column == LAYER - 1)
    peers = GRID - 1 + jnp.where(relays, 2, 0)
    for c in range(LAYER):
        linked = (column == c - 1) | (column == c + 1)
        if c in COLUMNS:
            linked = linked | ((relays if c in BETWEEN else at_end) & (column != c))
        peers = peers + jnp.where(linked, 1, 0)

        @pl.when(linked)
        def _():
            greet((layer + c, me))

    @pl.when(relays)
    def _():
        greet((lax.rem(blk + LAYER, blocks), me))
        greet((lax.rem(blk + blocks - LAYER, blocks), me))

    def message(field, device):
        return pl.ds(pl.multiple_of((field * GRID + device) * MSG, 8), MSG)

    def exchange(source, target, send_sem, recv_sem, field, peer):
        return pltpu.make_async_remote_copy(
            src_ref=source.at[message(field, peer)],
            dst_ref=target.at[message(field, me)],
            send_sem=send_sem.at[field, peer],
            recv_sem=recv_sem.at[field, me],
            device_id=(blk, peer),
            device_id_type=MESH,
        )

    def arrival(source, target, send_sem, recv_sem, field, peer):
        return pltpu.make_async_remote_copy(
            src_ref=source.at[message(field, peer)],
            dst_ref=target.at[message(field, peer)],
            send_sem=send_sem.at[field, peer],
            recv_sem=recv_sem.at[field, peer],
            device_id=(blk, peer),
            device_id_type=MESH,
        )

    def keep(source, target, field, way):
        here = message(field, me)
        return pltpu.make_async_copy(source.at[here], target.at[here], self_sem.at[way, field])

    def send_all(source, target, send_sem, recv_sem, field, way):
        for d in (4, 3, 5, 2, 6, 1, 7):
            exchange(source, target, send_sem, recv_sem, field, lax.rem(me + d, GRID)).start()
        keep(source, target, field, way).start()

    def await_all(source, target, send_sem, recv_sem, field, way):
        keep(source, target, field, way).wait()
        for d in range(1, GRID):
            peer = lax.rem(me + d, GRID)
            arrival(source, target, send_sem, recv_sem, field, peer).wait_recv()

    def band_rows(band):
        return pl.ds(pl.multiple_of(band * (SLAB * ROWS), 8), SLAB * ROWS)

    travel = ((band_out, band_in), (theirs_out, theirs_in))
    planes = SLAB // len(COLUMNS)

    def piece_rows(band, index):
        return pl.ds(pl.multiple_of((band * SLAB + index * planes) * ROWS, 8), planes * ROWS)

    def stop_rows(way, band):
        return pl.ds((way * 2 + band) * planes * ROWS, planes * ROWS)

    def to_block(way, band):
        source, target = travel[way]
        return pltpu.make_async_remote_copy(
            src_ref=source.at[band_rows(band)],
            dst_ref=target.at[band_rows(band)],
            send_sem=blk_send.at[way, band],
            recv_sem=blk_recv.at[way, band],
            device_id=((after, before)[way], me),
            device_id_type=MESH,
        )

    def to_column(way, band, index):
        return pltpu.make_async_remote_copy(
            src_ref=travel[way][0].at[piece_rows(band, index)],
            dst_ref=first_stop.at[stop_rows(way, band)],
            send_sem=first_send.at[way, band, index],
            recv_sem=first_recv.at[way, band],
            device_id=(layer + COLUMNS[index], me),
            device_id_type=MESH,
        )

    def along_column(way, band, start, end):
        source = first_stop.at[stop_rows(way, band)]
        if start:
            source = travel[way][0].at[piece_rows(band, COLUMNS.index(BETWEEN[way]))]
        target, done = second_stop.at[stop_rows(way, band)], second_recv.at[way, band]
        if end:
            index = COLUMNS.index(BETWEEN[1 - way])
            target = travel[way][1].at[piece_rows(band, index)]
            done = last_recv.at[way, band, index]
        next_layer = lax.rem(blk + (LAYER if way == 0 else blocks - LAYER), blocks)
        return pltpu.make_async_remote_copy(
            src_ref=source,
            dst_ref=target,
            send_sem=second_send.at[way, band],
            recv_sem=done,
            device_id=(next_layer, me),
            device_id_type=MESH,
        )

    def from_column(way, band, index):
        return pltpu.make_async_remote_copy(
            src_ref=second_stop.at[stop_rows(way, band)],
            dst_ref=travel[way][1].at[piece_rows(band, index)],
            send_sem=third_send.at[way, band],
            recv_sem=last_recv.at[way, band, index],
            device_id=(layer + BETWEEN[1 - way], me),
            device_id_type=MESH,
        )

    def depart(way, band):
        start = BETWEEN[way]

        @pl.when(column != start)
        def _():
            to_block(way, band).start()

        @pl.when(column == start)
        def _():
            along_column(way, band, True, False).start()
            for index, c in enumerate(COLUMNS):
                if c != start:
                    to_column(way, band, index).start()

    def relay_along(way, band):
        start, end = BETWEEN[way], BETWEEN[1 - way]

        @pl.when(relays & (column != start))
        def _():
            to_column(way, band, 0).wait_recv()

            @pl.when(column == end)
            def _():
                along_column(way, band, False, True).start()

            @pl.when(column != end)
            def _():
                along_column(way, band, False, False).start()

    def relay_in(way, band):
        @pl.when(relays & (column != BETWEEN[1 - way]))
        def _():
            along_column(way, band, False, False).wait_recv()
            from_column(way, band, piece).start()

    def arrive(way, band):
        end = BETWEEN[1 - way]

        @pl.when(column != end)
        def _():
            to_block(way, band).wait_recv()

        @pl.when(column == end)
        def _():
            for index in range(len(COLUMNS)):
                from_column(way, band, index).wait_recv()

    def departed(way, band):
        start, end = BETWEEN[way], BETWEEN[1 - way]

        @pl.when(column != start)
        def _():
            to_block(way, band).wait_send()

        @pl.when(column == start)
        def _():
            for index, c in enumerate(COLUMNS):
                if c != start:
                    to_column(way, band, index).wait_send()

        @pl.when(relays)
        def _():
            along_column(way, band, False, False).wait_send()

        @pl.when(relays & (column != end))
        def _():
            from_column(way, band, 0).wait_send()

    def put_packed(ref, band, x, plane):
        start = pl.multiple_of((band * SLAB + x) * ROWS, 8)
        for k, part in enumerate(pack(plane)):
            ref[pl.ds(start + 24 * k, 24), :] = part

    def get_packed(ref, band, x):
        start = pl.multiple_of((band * SLAB + x) * ROWS, 8)
        return unpack([ref[pl.ds(start + 24 * k, 24), :] for k in range(3)])

    for band in range(2):

        @pl.loop(0, SLAB)
        def _(x):
            plane = own_ref[band, x]
            bands[band, x] = plane
            put_packed(band_out, band, x, plane)

    pl.semaphore_wait(barrier, peers)
    for band in range(2):
        depart(0, band)

    acc[...] = jnp.zeros_like(acc)

    def pair(field):
        first = jnp.where(field < 3, field // 2, (field + 1) % 2)
        second = jnp.where(field < 3, (field + 1) // 2, 2 + (field - 3) // 2)
        return first, second

    def forward(field):
        first, second = pair(field)
        for group in range(0, SLAB, 4):
            density = bands[first, pl.ds(group, 4)] * bands[second, pl.ds(group, 4)]
            along_z = from_right(density.reshape(4 * NG, NG), right_ref)
            for i in range(4):
                plane = from_left(plane_ref[...], along_z[i * NG : (i + 1) * NG])
                parts = pack(plane)
                for t in range(TILES):
                    tile = parts[t // 3][t % 3 * 8 : t % 3 * 8 + 8]
                    sent[
                        pl.ds(field * (GRID * MSG) + t * SLAB + group + i, GRID, stride=MSG), :
                    ] = tile
        send_all(sent, got, fwd_send, fwd_recv, field, 0)

    def make_coulomb():
        factor = 4.0 * np.pi / (2.0 * np.pi / BOX_EDGE) ** 2 / float(NG) ** 3

        def square(index):
            folded = jnp.minimum(index, NG - index)
            return folded * folded

        kx = lax.broadcasted_iota(jnp.int32, (NG, 128), 0)
        lane = lax.broadcasted_iota(jnp.int32, (NG, 128), 1)

        @pl.loop(0, TILES)
        def _(t):
            row = t * GRID + me
            part, a = row // 24, row % 24
            ky = jnp.where(lane < NG, 24 * part + a, 72 + a)
            kz = jnp.where(lane < NG, lane, 32 * part + lane - NG)
            total = square(kx) + square(ky) + square(kz)
            safe = jnp.maximum(total, 1).astype(F32)
            coulomb[t] = jnp.where(total > 0, factor / safe, 0.0)

    def solve(field):
        await_all(sent, got, fwd_send, fwd_recv, field, 0)
        base = field * (GRID * MSG)
        for t in range(TILES):
            column = jnp.concatenate(
                [
                    got[pl.ds(base + t * SLAB + x, GRID, stride=MSG), :]
                    for x in range(SLAB)
                ],
                axis=0,
            )
            spectrum = from_left(there_ref[...], column) * coulomb[t]
            mixed = from_left(back_ref[...], spectrum)
            for x in range(SLAB):
                ret_sent[pl.ds(base + t * SLAB + x, GRID, stride=MSG), :] = mixed[
                    x * GRID : (x + 1) * GRID
                ]
        send_all(ret_sent, ret_got, bwd_send, bwd_recv, field, 1)

    def backward(field):
        await_all(ret_sent, ret_got, bwd_send, bwd_recv, field, 1)
        first, second = pair(field)
        base = field * (GRID * MSG)
        for group in range(0, SLAB, 4):
            planes = []
            for i in range(4):
                tiles = [
                    ret_got[pl.ds(base + t * SLAB + group + i, GRID, stride=MSG), :]
                    for t in range(TILES)
                ]
                parts = [jnp.concatenate(tiles[3 * k : 3 * k + 3], axis=0) for k in range(3)]
                planes.append(from_left(plane_ref[...], unpack(parts)))
            potential = from_right(jnp.concatenate(planes, axis=0), right_ref)
            potential = potential.reshape(4, NG, NG)
            here = pl.ds(group, 4)
            acc[first, here] += potential * bands[second, here]

            @pl.when(first != second)
            def _():
                acc[second, here] += potential * bands[first, here]

    def give_back(band):
        @pl.loop(0, SLAB)
        def _(x):
            put_packed(theirs_out, band, x, acc[2 + band, x])

        depart(1, band)

    def at(step, fields):
        return sum(jnp.where(step == i, field, 0) for i, field in enumerate(fields))

    @pl.loop(0, len(FORWARD))
    def _(step):
        @pl.when(step == 2)
        def _():
            for band in range(2):
                relay_along(0, band)

        @pl.when(step == 3)
        def _():
            for band in range(2):
                relay_in(0, band)
            for band in range(2):
                arrive(0, band)

                @pl.loop(0, SLAB)
                def _(x):
                    bands[2 + band, x] = get_packed(band_in, band, x)

        forward_field = at(step, FORWARD)

        @pl.when(forward_field >= 0)
        def _():
            forward(forward_field)

        @pl.when(step == 2)
        def _():
            make_coulomb()

        solve_field = at(step, SOLVE)

        @pl.when(solve_field >= 0)
        def _():
            solve(solve_field)

        @pl.when(step == 12)
        def _():
            relay_in(1, 0)

        @pl.when(step == 14)
        def _():
            relay_in(1, 1)

        backward_field = at(step, BACKWARD)

        @pl.when(backward_field >= 0)
        def _():
            backward(backward_field)

        @pl.when(step == 10)
        def _():
            give_back(0)

        @pl.when(step == 11)
        def _():
            relay_along(1, 0)

        @pl.when(step == 12)
        def _():
            give_back(1)

        @pl.when(step == 13)
        def _():
            relay_along(1, 1)

    for band in range(2):
        arrive(1, band)

        @pl.loop(0, SLAB)
        def _(x):
            out_ref[band, x] = -(acc[band, x] + get_packed(theirs_in, band, x))

    @pl.loop(0, FIELDS)
    def _(field):
        for d in range(1, GRID):
            peer = lax.rem(me + d, GRID)
            exchange(sent, got, fwd_send, fwd_recv, field, peer).wait_send()
            exchange(ret_sent, ret_got, bwd_send, bwd_recv, field, peer).wait_send()

    for band in range(2):
        for way in range(2):
            departed(way, band)


def body(blocks, bands):
    count, slab, plane = bands.shape
    own = bands.reshape(count, slab, NG, NG)
    constants = [jnp.asarray(table) for table in tables()]
    vmem = pl.BlockSpec(memory_space=pltpu.VMEM)
    messages = pltpu.VMEM((FIELDS * GRID * MSG, 128), F32)
    packed = pltpu.VMEM((count * SLAB * ROWS, 128), F32)
    stops = pltpu.VMEM((2 * count * (SLAB // len(COLUMNS)) * ROWS, 128), F32)
    out = pl.pallas_call(
        functools.partial(kernel, blocks),
        out_shape=jax.ShapeDtypeStruct((count, slab, NG, NG), F32),
        in_specs=[vmem] * 5,
        out_specs=vmem,
        scratch_shapes=[
            pltpu.VMEM((2 * count, SLAB, NG, NG), F32),
            pltpu.VMEM((2 * count, SLAB, NG, NG), F32),
            pltpu.VMEM((TILES, NG, 128), F32),
            messages,
            messages,
            messages,
            messages,
            packed,
            packed,
            packed,
            packed,
            pltpu.SemaphoreType.DMA((FIELDS, GRID)),
            pltpu.SemaphoreType.DMA((FIELDS, GRID)),
            pltpu.SemaphoreType.DMA((FIELDS, GRID)),
            pltpu.SemaphoreType.DMA((FIELDS, GRID)),
            pltpu.SemaphoreType.DMA((2, FIELDS)),
            pltpu.SemaphoreType.DMA((2, 2)),
            pltpu.SemaphoreType.DMA((2, 2)),
            stops,
            stops,
            pltpu.SemaphoreType.DMA((2, 2, len(COLUMNS))),
            pltpu.SemaphoreType.DMA((2, 2)),
            pltpu.SemaphoreType.DMA((2, 2)),
            pltpu.SemaphoreType.DMA((2, 2)),
            pltpu.SemaphoreType.DMA((2, 2)),
            pltpu.SemaphoreType.DMA((2, 2, len(COLUMNS))),
        ],
        compiler_params=pltpu.CompilerParams(
            collective_id=0, has_side_effects=True, vmem_limit_bytes=48 * 1024 * 1024
        ),
    )(own, *constants)
    return out.reshape(count, slab, plane)


def solution(mesh):
    spec = P("blk", "grid", None)
    return jax.shard_map(
        functools.partial(body, mesh.shape["blk"]),
        mesh=mesh,
        in_specs=(spec,),
        out_specs=spec,
        check_vma=False,
    )
```

```python
import functools

import jax
import jax.numpy as jnp
import ml_dtypes
import numpy as np
from jax import lax
from jax.experimental import pallas as pl
from jax.experimental.pallas import tpu as pltpu
from jax.sharding import PartitionSpec as P

NG = 96
BOX_EDGE = 23.47
MESH = pl.DeviceIdType.MESH
F32 = jnp.float32
BF16 = jnp.bfloat16

GRID = 8
SLAB = NG // GRID
ROWS = NG * NG // 128
TILES = ROWS // GRID
MSG = 112
FIELDS = 7

LAYER = 16
COLUMNS = (0, 1, 2, 3, 4, 7, 8, 11, 12, 13, 14, 15)
BETWEEN = LAYER - 1, 0

FORWARD = (0, 1, 2, 3, 4, 5, 6, -1, -1, -1, -1, -1, -1, -1, -1, -1)
SOLVE = (-1, -1, -1, -1, -1, -1, -1, 3, 4, 5, 6, 0, 1, 2, -1, -1)
BACKWARD = (-1, -1, -1, -1, -1, -1, -1, -1, -1, 3, 4, 5, 6, 0, 1, 2)


def hartley(rows, cols):
    angle = (rows[:, None] * cols[None, :] % NG) * (2.0 * np.pi / NG)
    return np.cos(angle) + np.sin(angle)


def split_table(table):
    parts = []
    for _ in range(3):
        part = table.astype(np.float32).astype(ml_dtypes.bfloat16)
        parts.append(part)
        table = table - part.astype(np.float64)
    return parts


def left_table(table):
    return np.concatenate([np.concatenate([part, part], axis=1) for part in split_table(table)])


def right_table(table):
    parts = [np.pad(part, ((0, 0), (0, 128 - NG))) for part in split_table(table)]
    return np.concatenate(parts, axis=1)


def tables():
    plain = np.arange(NG)
    mixed = np.arange(NG) % GRID * SLAB + np.arange(NG) // GRID
    return (
        right_table(hartley(plain, plain)),
        left_table(hartley(plain, plain)),
        left_table(hartley(plain, mixed)),
        left_table(hartley(mixed, plain)),
    )


def split(value):
    high = value.astype(BF16)
    low = (value - high.astype(F32)).astype(BF16)
    return high, low


def dot(a, b):
    return jnp.dot(a, b, preferred_element_type=F32)


def from_left(table, value):
    high, low = split(value)
    both = dot(table, jnp.concatenate([high, low], axis=0))
    return both[:NG] + (both[NG : 2 * NG] + both[2 * NG :])


def from_right(value, right_ref):
    high, low = split(value)
    above = dot(high, right_ref[:, :256])
    below = dot(low, right_ref[:, :256])
    rest = dot(high, right_ref[:, 256:])
    second = above[:, 128 : 128 + NG] + below[:, :NG]
    return above[:, :NG] + (second + (below[:, 128 : 128 + NG] + rest[:, :NG]))


def pack(plane):
    last = plane[72:96]
    return [
        jnp.concatenate([plane[24 * k : 24 * k + 24], last[:, 32 * k : 32 * k + 32]], axis=1)
        for k in range(3)
    ]


def unpack(parts):
    last = jnp.concatenate([part[:, 96:128] for part in parts], axis=1)
    return jnp.concatenate([part[:, :96] for part in parts] + [last], axis=0)


def kernel(
    blocks,
    own_ref,
    right_ref,
    plane_ref,
    there_ref,
    back_ref,
    out_ref,
    bands,
    acc,
    coulomb,
    sent,
    got,
    ret_sent,
    ret_got,
    band_out,
    band_in,
    theirs_out,
    theirs_in,
    fwd_send,
    fwd_recv,
    bwd_send,
    bwd_recv,
    self_sem,
    blk_send,
    blk_recv,
    first_stop,
    second_stop,
    first_send,
    first_recv,
    second_send,
    second_recv,
    third_send,
    last_recv,
):
    blk = lax.axis_index("blk")
    me = lax.axis_index("grid")
    after = lax.rem(blk + 1, blocks)
    before = lax.rem(blk + blocks - 1, blocks)

    column = lax.rem(blk, LAYER)
    layer = blk - column
    piece = sum(jnp.where(column == c, i, 0) for i, c in enumerate(COLUMNS))
    relays = functools.reduce(jnp.logical_or, [column == c for c in COLUMNS])

    barrier = pltpu.get_barrier_semaphore()

    def greet(other):
        pl.semaphore_signal(barrier, inc=1, device_id=other, device_id_type=MESH)

    for d in range(1, GRID):
        greet((blk, lax.rem(me + d, GRID)))

    at_end = (column == 0) | (column == LAYER - 1)
    peers = GRID - 1 + jnp.where(relays, 2, 0)
    for c in range(LAYER):
        linked = (column == c - 1) | (column == c + 1)
        if c in COLUMNS:
            linked = linked | ((relays if c in BETWEEN else at_end) & (column != c))
        peers = peers + jnp.where(linked, 1, 0)

        @pl.when(linked)
        def _():
            greet((layer + c, me))

    @pl.when(relays)
    def _():
        greet((lax.rem(blk + LAYER, blocks), me))
        greet((lax.rem(blk + blocks - LAYER, blocks), me))

    def message(field, device):
        return pl.ds(pl.multiple_of((field * GRID + device) * MSG, 8), MSG)

    def exchange(source, target, send_sem, recv_sem, field, peer):
        return pltpu.make_async_remote_copy(
            src_ref=source.at[message(field, peer)],
            dst_ref=target.at[message(field, me)],
            send_sem=send_sem.at[field, peer],
            recv_sem=recv_sem.at[field, me],
            device_id=(blk, peer),
            device_id_type=MESH,
        )

    def arrival(source, target, send_sem, recv_sem, field, peer):
        return pltpu.make_async_remote_copy(
            src_ref=source.at[message(field, peer)],
            dst_ref=target.at[message(field, peer)],
            send_sem=send_sem.at[field, peer],
            recv_sem=recv_sem.at[field, peer],
            device_id=(blk, peer),
            device_id_type=MESH,
        )

    def keep(source, target, field, way):
        here = message(field, me)
        return pltpu.make_async_copy(source.at[here], target.at[here], self_sem.at[way, field])

    def send_all(source, target, send_sem, recv_sem, field, way):
        for d in (4, 3, 5, 2, 6, 1, 7):
            exchange(source, target, send_sem, recv_sem, field, lax.rem(me + d, GRID)).start()
        keep(source, target, field, way).start()

    def await_all(source, target, send_sem, recv_sem, field, way):
        keep(source, target, field, way).wait()
        for d in range(1, GRID):
            peer = lax.rem(me + d, GRID)
            arrival(source, target, send_sem, recv_sem, field, peer).wait_recv()

    def band_rows(band):
        return pl.ds(pl.multiple_of(band * (SLAB * ROWS), 8), SLAB * ROWS)

    travel = ((band_out, band_in), (theirs_out, theirs_in))
    planes = SLAB // len(COLUMNS)

    def piece_rows(band, index):
        return pl.ds(pl.multiple_of((band * SLAB + index * planes) * ROWS, 8), planes * ROWS)

    def stop_rows(way, band):
        return pl.ds((way * 2 + band) * planes * ROWS, planes * ROWS)

    def to_block(way, band):
        source, target = travel[way]
        return pltpu.make_async_remote_copy(
            src_ref=source.at[band_rows(band)],
            dst_ref=target.at[band_rows(band)],
            send_sem=blk_send.at[way, band],
            recv_sem=blk_recv.at[way, band],
            device_id=((after, before)[way], me),
            device_id_type=MESH,
        )

    def to_column(way, band, index):
        return pltpu.make_async_remote_copy(
            src_ref=travel[way][0].at[piece_rows(band, index)],
            dst_ref=first_stop.at[stop_rows(way, band)],
            send_sem=first_send.at[way, band, index],
            recv_sem=first_recv.at[way, band],
            device_id=(layer + COLUMNS[index], me),
            device_id_type=MESH,
        )

    def along_column(way, band, start, end):
        source = first_stop.at[stop_rows(way, band)]
        if start:
            source = travel[way][0].at[piece_rows(band, COLUMNS.index(BETWEEN[way]))]
        target, done = second_stop.at[stop_rows(way, band)], second_recv.at[way, band]
        if end:
            index = COLUMNS.index(BETWEEN[1 - way])
            target = travel[way][1].at[piece_rows(band, index)]
            done = last_recv.at[way, band, index]
        next_layer = lax.rem(blk + (LAYER if way == 0 else blocks - LAYER), blocks)
        return pltpu.make_async_remote_copy(
            src_ref=source,
            dst_ref=target,
            send_sem=second_send.at[way, band],
            recv_sem=done,
            device_id=(next_layer, me),
            device_id_type=MESH,
        )

    def from_column(way, band, index):
        return pltpu.make_async_remote_copy(
            src_ref=second_stop.at[stop_rows(way, band)],
            dst_ref=travel[way][1].at[piece_rows(band, index)],
            send_sem=third_send.at[way, band],
            recv_sem=last_recv.at[way, band, index],
            device_id=(layer + BETWEEN[1 - way], me),
            device_id_type=MESH,
        )

    def depart(way, band):
        start = BETWEEN[way]

        @pl.when(column != start)
        def _():
            to_block(way, band).start()

        @pl.when(column == start)
        def _():
            along_column(way, band, True, False).start()
            for index, c in enumerate(COLUMNS):
                if c != start:
                    to_column(way, band, index).start()

    def relay_along(way, band):
        start, end = BETWEEN[way], BETWEEN[1 - way]

        @pl.when(relays & (column != start))
        def _():
            to_column(way, band, 0).wait_recv()

            @pl.when(column == end)
            def _():
                along_column(way, band, False, True).start()

            @pl.when(column != end)
            def _():
                along_column(way, band, False, False).start()

    def relay_in(way, band):
        @pl.when(relays & (column != BETWEEN[1 - way]))
        def _():
            along_column(way, band, False, False).wait_recv()
            from_column(way, band, piece).start()

    def arrive(way, band):
        end = BETWEEN[1 - way]

        @pl.when(column != end)
        def _():
            to_block(way, band).wait_recv()

        @pl.when(column == end)
        def _():
            for index in range(len(COLUMNS)):
                from_column(way, band, index).wait_recv()

    def departed(way, band):
        start, end = BETWEEN[way], BETWEEN[1 - way]

        @pl.when(column != start)
        def _():
            to_block(way, band).wait_send()

        @pl.when(column == start)
        def _():
            for index, c in enumerate(COLUMNS):
                if c != start:
                    to_column(way, band, index).wait_send()

        @pl.when(relays)
        def _():
            along_column(way, band, False, False).wait_send()

        @pl.when(relays & (column != end))
        def _():
            from_column(way, band, 0).wait_send()

    def put_packed(ref, band, x, plane):
        start = pl.multiple_of((band * SLAB + x) * ROWS, 8)
        for k, part in enumerate(pack(plane)):
            ref[pl.ds(start + 24 * k, 24), :] = part

    def get_packed(ref, band, x):
        start = pl.multiple_of((band * SLAB + x) * ROWS, 8)
        return unpack([ref[pl.ds(start + 24 * k, 24), :] for k in range(3)])

    for band in range(2):

        @pl.loop(0, SLAB)
        def _(x):
            plane = own_ref[band, x]
            bands[band, x] = plane
            put_packed(band_out, band, x, plane)

    pl.semaphore_wait(barrier, peers)
    for band in range(2):
        depart(0, band)

    acc[...] = jnp.zeros_like(acc)

    def pair(field):
        first = jnp.where(field < 3, field // 2, (field + 1) % 2)
        second = jnp.where(field < 3, (field + 1) // 2, 2 + (field - 3) // 2)
        return first, second

    def forward(field):
        first, second = pair(field)
        for group in range(0, SLAB, 4):
            density = bands[first, pl.ds(group, 4)] * bands[second, pl.ds(group, 4)]
            along_z = from_right(density.reshape(4 * NG, NG), right_ref)
            for i in range(4):
                plane = from_left(plane_ref[...], along_z[i * NG : (i + 1) * NG])
                parts = pack(plane)
                for t in range(TILES):
                    tile = parts[t // 3][t % 3 * 8 : t % 3 * 8 + 8]
                    sent[
                        pl.ds(field * (GRID * MSG) + t * SLAB + group + i, GRID, stride=MSG), :
                    ] = tile

    def make_coulomb():
        factor = 4.0 * np.pi / (2.0 * np.pi / BOX_EDGE) ** 2 / float(NG) ** 3

        def square(index):
            folded = jnp.minimum(index, NG - index)
            return folded * folded

        kx = lax.broadcasted_iota(jnp.int32, (NG, 128), 0)
        lane = lax.broadcasted_iota(jnp.int32, (NG, 128), 1)

        @pl.loop(0, TILES)
        def _(t):
            row = t * GRID + me
            part, a = row // 24, row % 24
            ky = jnp.where(lane < NG, 24 * part + a, 72 + a)
            kz = jnp.where(lane < NG, lane, 32 * part + lane - NG)
            total = square(kx) + square(ky) + square(kz)
            safe = jnp.maximum(total, 1).astype(F32)
            coulomb[t] = jnp.where(total > 0, factor / safe, 0.0)

    def solve(field):
        await_all(sent, got, fwd_send, fwd_recv, field, 0)
        base = field * (GRID * MSG)
        for t in range(TILES):
            column = jnp.concatenate(
                [
                    got[pl.ds(base + t * SLAB + x, GRID, stride=MSG), :]
                    for x in range(SLAB)
                ],
                axis=0,
            )
            spectrum = from_left(there_ref[...], column) * coulomb[t]
            mixed = from_left(back_ref[...], spectrum)
            for x in range(SLAB):
                ret_sent[pl.ds(base + t * SLAB + x, GRID, stride=MSG), :] = mixed[
                    x * GRID : (x + 1) * GRID
                ]
        send_all(ret_sent, ret_got, bwd_send, bwd_recv, field, 1)

    def backward(field):
        await_all(ret_sent, ret_got, bwd_send, bwd_recv, field, 1)
        first, second = pair(field)
        base = field * (GRID * MSG)
        for group in range(0, SLAB, 4):
            planes = []
            for i in range(4):
                tiles = [
                    ret_got[pl.ds(base + t * SLAB + group + i, GRID, stride=MSG), :]
                    for t in range(TILES)
                ]
                parts = [jnp.concatenate(tiles[3 * k : 3 * k + 3], axis=0) for k in range(3)]
                planes.append(from_left(plane_ref[...], unpack(parts)))
            potential = from_right(jnp.concatenate(planes, axis=0), right_ref)
            potential = potential.reshape(4, NG, NG)
            here = pl.ds(group, 4)
            acc[first, here] += potential * bands[second, here]

            @pl.when(first != second)
            def _():
                acc[second, here] += potential * bands[first, here]

    def give_back(band):
        @pl.loop(0, SLAB)
        def _(x):
            put_packed(theirs_out, band, x, acc[2 + band, x])

        depart(1, band)

    def at(step, fields):
        return sum(jnp.where(step == i, field, 0) for i, field in enumerate(fields))

    @pl.loop(0, len(FORWARD))
    def _(step):
        @pl.when(step == 3)
        def _():
            for band in range(2):
                arrive(0, band)

                @pl.loop(0, SLAB)
                def _(x):
                    bands[2 + band, x] = get_packed(band_in, band, x)

        forward_field = at(step, FORWARD)

        @pl.when(forward_field >= 0)
        def _():
            forward(forward_field)

        @pl.when(step == 0)
        def _():
            for band in range(2):
                relay_along(0, band)

        @pl.when(step == 1)
        def _():
            for band in range(2):
                relay_in(0, band)

        @pl.when(forward_field >= 0)
        def _():
            send_all(sent, got, fwd_send, fwd_recv, forward_field, 0)

        @pl.when(step == 2)
        def _():
            make_coulomb()

        solve_field = at(step, SOLVE)
        backward_field = at(step, BACKWARD)

        @pl.when((solve_field >= 0) & (step < 12))
        def _():
            solve(solve_field)

        @pl.when(backward_field >= 0)
        def _():
            backward(backward_field)

        @pl.when(step == 10)
        def _():
            give_back(0)

        @pl.when(step == 12)
        def _():
            give_back(1)
            relay_along(1, 0)

        @pl.when(step == 13)
        def _():
            relay_along(1, 1)
            relay_in(1, 0)

        @pl.when(step == 14)
        def _():
            relay_in(1, 1)

        @pl.when((solve_field >= 0) & (step >= 12))
        def _():
            solve(solve_field)

    for band in range(2):
        arrive(1, band)

        @pl.loop(0, SLAB)
        def _(x):
            out_ref[band, x] = -(acc[band, x] + get_packed(theirs_in, band, x))

    @pl.loop(0, FIELDS)
    def _(field):
        for d in range(1, GRID):
            peer = lax.rem(me + d, GRID)
            exchange(sent, got, fwd_send, fwd_recv, field, peer).wait_send()
            exchange(ret_sent, ret_got, bwd_send, bwd_recv, field, peer).wait_send()

    for band in range(2):
        for way in range(2):
            departed(way, band)


def body(blocks, bands):
    count, slab, plane = bands.shape
    own = bands.reshape(count, slab, NG, NG)
    constants = [jnp.asarray(table) for table in tables()]
    vmem = pl.BlockSpec(memory_space=pltpu.VMEM)
    messages = pltpu.VMEM((FIELDS * GRID * MSG, 128), F32)
    packed = pltpu.VMEM((count * SLAB * ROWS, 128), F32)
    stops = pltpu.VMEM((2 * count * (SLAB // len(COLUMNS)) * ROWS, 128), F32)
    out = pl.pallas_call(
        functools.partial(kernel, blocks),
        out_shape=jax.ShapeDtypeStruct((count, slab, NG, NG), F32),
        in_specs=[vmem] * 5,
        out_specs=vmem,
        scratch_shapes=[
            pltpu.VMEM((2 * count, SLAB, NG, NG), F32),
            pltpu.VMEM((2 * count, SLAB, NG, NG), F32),
            pltpu.VMEM((TILES, NG, 128), F32),
            messages,
            messages,
            messages,
            messages,
            packed,
            packed,
            packed,
            packed,
            pltpu.SemaphoreType.DMA((FIELDS, GRID)),
            pltpu.SemaphoreType.DMA((FIELDS, GRID)),
            pltpu.SemaphoreType.DMA((FIELDS, GRID)),
            pltpu.SemaphoreType.DMA((FIELDS, GRID)),
            pltpu.SemaphoreType.DMA((2, FIELDS)),
            pltpu.SemaphoreType.DMA((2, 2)),
            pltpu.SemaphoreType.DMA((2, 2)),
            stops,
            stops,
            pltpu.SemaphoreType.DMA((2, 2, len(COLUMNS))),
            pltpu.SemaphoreType.DMA((2, 2)),
            pltpu.SemaphoreType.DMA((2, 2)),
            pltpu.SemaphoreType.DMA((2, 2)),
            pltpu.SemaphoreType.DMA((2, 2)),
            pltpu.SemaphoreType.DMA((2, 2, len(COLUMNS))),
        ],
        compiler_params=pltpu.CompilerParams(
            collective_id=0, has_side_effects=True, vmem_limit_bytes=48 * 1024 * 1024
        ),
    )(own, *constants)
    return out.reshape(count, slab, plane)


def solution(mesh):
    spec = P("blk", "grid", None)
    return jax.shard_map(
        functools.partial(body, mesh.shape["blk"]),
        mesh=mesh,
        in_specs=(spec,),
        out_specs=spec,
        check_vma=False,
    )
```

```python
import functools

import jax
import jax.numpy as jnp
import ml_dtypes
import numpy as np
from jax import lax
from jax.experimental import pallas as pl
from jax.experimental.pallas import tpu as pltpu
from jax.sharding import PartitionSpec as P

NG = 96
BOX_EDGE = 23.47
MESH = pl.DeviceIdType.MESH
F32 = jnp.float32
BF16 = jnp.bfloat16

GRID = 8
SLAB = NG // GRID
ROWS = NG * NG // 128
SHARE = 8, 10
MSG = SHARE[1] * SLAB
FIELDS = 7

LAYER = 16
COLUMNS = (0, 1, 2, 3, 4, 7, 8, 11, 12, 13, 14, 15)
BETWEEN = LAYER - 1, 0

FORWARD = (0, 1, 2, 3, 4, 5, 6, -1, -1, -1, -1, -1, -1, -1, -1, -1)
SOLVE = (-1, -1, -1, -1, -1, -1, -1, 3, 4, 5, 6, 0, 1, 2, -1, -1)
BACKWARD = (-1, -1, -1, -1, -1, -1, -1, -1, -1, 3, 4, 5, 6, 0, 1, 2)


def hartley(rows, cols):
    angle = (rows[:, None] * cols[None, :] % NG) * (2.0 * np.pi / NG)
    return np.cos(angle) + np.sin(angle)


def split_table(table):
    parts = []
    for _ in range(3):
        part = table.astype(np.float32).astype(ml_dtypes.bfloat16)
        parts.append(part)
        table = table - part.astype(np.float64)
    return parts


def left_table(table):
    return np.concatenate([np.concatenate([part, part], axis=1) for part in split_table(table)])


def right_table(table):
    parts = [np.pad(part, ((0, 0), (0, 128 - NG))) for part in split_table(table)]
    return np.concatenate(parts, axis=1)


def tables():
    plain = np.arange(NG)
    mixed = np.arange(NG) % GRID * SLAB + np.arange(NG) // GRID
    return (
        right_table(hartley(plain, plain)),
        left_table(hartley(plain, plain)),
        left_table(hartley(plain, mixed)),
        left_table(hartley(mixed, plain)),
    )


def split(value):
    high = value.astype(BF16)
    low = (value - high.astype(F32)).astype(BF16)
    return high, low


def dot(a, b):
    return jnp.dot(a, b, preferred_element_type=F32)


def from_left(table, value):
    high, low = split(value)
    both = dot(table, jnp.concatenate([high, low], axis=0))
    return both[:NG] + (both[NG : 2 * NG] + both[2 * NG :])


def from_right(value, right_ref):
    high, low = split(value)
    above = dot(high, right_ref[:, :256])
    below = dot(low, right_ref[:, :256])
    rest = dot(high, right_ref[:, 256:])
    second = above[:, 128 : 128 + NG] + below[:, :NG]
    return above[:, :NG] + (second + (below[:, 128 : 128 + NG] + rest[:, :NG]))


def pack(plane):
    last = plane[72:96]
    return [
        jnp.concatenate([plane[24 * k : 24 * k + 24], last[:, 32 * k : 32 * k + 32]], axis=1)
        for k in range(3)
    ]


def unpack(parts):
    last = jnp.concatenate([part[:, 96:128] for part in parts], axis=1)
    return jnp.concatenate([part[:, :96] for part in parts] + [last], axis=0)


def kernel(
    blocks,
    own_ref,
    right_ref,
    plane_ref,
    there_ref,
    back_ref,
    out_ref,
    bands,
    acc,
    coulomb,
    sent,
    got,
    ret_sent,
    ret_got,
    band_out,
    band_in,
    theirs_out,
    theirs_in,
    fwd_send,
    fwd_recv,
    bwd_send,
    bwd_recv,
    self_sem,
    blk_send,
    blk_recv,
    stop,
    first_send,
    stop_recv,
    second_send,
    last_recv,
):
    blk = lax.axis_index("blk")
    me = lax.axis_index("grid")
    after = lax.rem(blk + 1, blocks)
    before = lax.rem(blk + blocks - 1, blocks)

    column = lax.rem(blk, LAYER)
    layer = blk - column
    piece = sum(jnp.where(column == c, i, 0) for i, c in enumerate(COLUMNS))
    relays = functools.reduce(jnp.logical_or, [column == c for c in COLUMNS])

    barrier = pltpu.get_barrier_semaphore()

    def greet(other):
        pl.semaphore_signal(barrier, inc=1, device_id=other, device_id_type=MESH)

    for d in range(1, GRID):
        greet((blk, lax.rem(me + d, GRID)))

    at_end = (column == 0) | (column == LAYER - 1)
    peers = GRID - 1 + jnp.where(relays, jnp.where(at_end, len(COLUMNS) + 1, 2), 0)
    for c in range(LAYER):
        linked = (column == c - 1) | (column == c + 1)
        if c in COLUMNS:
            linked = linked | ((relays if c in BETWEEN else at_end) & (column != c))
        peers = peers + jnp.where(linked, 1, 0)

        @pl.when(linked)
        def _():
            greet((layer + c, me))

    def other_layer(way):
        return lax.rem(layer + (LAYER if way == 0 else blocks - LAYER), blocks)

    for way, end in enumerate(BETWEEN):

        @pl.when(column == end)
        def _():
            for c in COLUMNS:
                greet((other_layer(way) + c, me))

        @pl.when(relays & (column != BETWEEN[1 - way]))
        def _():
            greet((other_layer(1 - way) + end, me))

    def message(field, device, share):
        return pl.ds(pl.multiple_of((field * GRID + device) * MSG, 8), share * SLAB)

    def exchange(source, target, send_sem, recv_sem, field, peer, share):
        return pltpu.make_async_remote_copy(
            src_ref=source.at[message(field, peer, share)],
            dst_ref=target.at[message(field, me, share)],
            send_sem=send_sem.at[field, peer],
            recv_sem=recv_sem.at[field, me],
            device_id=(blk, peer),
            device_id_type=MESH,
        )

    def arrival(source, target, send_sem, recv_sem, field, peer, share):
        return pltpu.make_async_remote_copy(
            src_ref=source.at[message(field, peer, share)],
            dst_ref=target.at[message(field, peer, share)],
            send_sem=send_sem.at[field, peer],
            recv_sem=recv_sem.at[field, peer],
            device_id=(blk, peer),
            device_id_type=MESH,
        )

    def keep(source, target, field, way, share):
        here = message(field, me, share)
        return pltpu.make_async_copy(source.at[here], target.at[here], self_sem.at[way, field])

    buffers = ((sent, got, fwd_send, fwd_recv), (ret_sent, ret_got, bwd_send, bwd_recv))

    def by_parity(run):
        for parity in range(2):

            @pl.when(me % 2 == parity)
            def _():
                run(parity)

    def send_all(field, way):
        def run(parity):
            for d in (4, 3, 5, 2, 6, 1, 7):
                share = SHARE[parity if way else (parity + d) % 2]
                exchange(*buffers[way], field, lax.rem(me + d, GRID), share).start()
            keep(*buffers[way][:2], field, way, SHARE[parity]).start()

        by_parity(run)

    def await_all(field, way):
        def run(parity):
            keep(*buffers[way][:2], field, way, SHARE[parity]).wait()
            for d in range(1, GRID):
                share = SHARE[(parity + d) % 2 if way else parity]
                arrival(*buffers[way], field, lax.rem(me + d, GRID), share).wait_recv()

        by_parity(run)

    def await_sent(field, way):
        def run(parity):
            for d in range(1, GRID):
                share = SHARE[parity if way else (parity + d) % 2]
                exchange(*buffers[way], field, lax.rem(me + d, GRID), share).wait_send()

        by_parity(run)

    def band_rows(band):
        return pl.ds(pl.multiple_of(band * (SLAB * ROWS), 8), SLAB * ROWS)

    travel = ((band_out, band_in), (theirs_out, theirs_in))
    planes = SLAB // len(COLUMNS)

    def piece_rows(band, index):
        return pl.ds(pl.multiple_of((band * SLAB + index * planes) * ROWS, 8), planes * ROWS)

    def stop_rows(way, band):
        return pl.ds((way * 2 + band) * planes * ROWS, planes * ROWS)

    def to_block(way, band):
        source, target = travel[way]
        return pltpu.make_async_remote_copy(
            src_ref=source.at[band_rows(band)],
            dst_ref=target.at[band_rows(band)],
            send_sem=blk_send.at[way, band],
            recv_sem=blk_recv.at[way, band],
            device_id=((after, before)[way], me),
            device_id_type=MESH,
        )

    def to_column(way, band, index):
        target, done = stop.at[stop_rows(way, band)], stop_recv.at[way, band]
        if COLUMNS[index] == BETWEEN[1 - way]:
            target = travel[way][1].at[piece_rows(band, index)]
            done = last_recv.at[way, band, index]
        return pltpu.make_async_remote_copy(
            src_ref=travel[way][0].at[piece_rows(band, index)],
            dst_ref=target,
            send_sem=first_send.at[way, band, index],
            recv_sem=done,
            device_id=(other_layer(way) + COLUMNS[index], me),
            device_id_type=MESH,
        )

    def from_column(way, band, index):
        return pltpu.make_async_remote_copy(
            src_ref=stop.at[stop_rows(way, band)],
            dst_ref=travel[way][1].at[piece_rows(band, index)],
            send_sem=second_send.at[way, band],
            recv_sem=last_recv.at[way, band, index],
            device_id=(layer + BETWEEN[1 - way], me),
            device_id_type=MESH,
        )

    def depart(way, band):
        start = BETWEEN[way]

        @pl.when(column != start)
        def _():
            to_block(way, band).start()

        @pl.when(column == start)
        def _():
            for index in range(len(COLUMNS)):
                to_column(way, band, index).start()

    def relay_in(way, band):
        end = BETWEEN[1 - way]
        inner = COLUMNS.index(BETWEEN[way])

        @pl.when(relays & (column != end))
        def _():
            to_column(way, band, inner).wait_recv()
            from_column(way, band, piece).start()

    def arrive(way, band):
        end = BETWEEN[1 - way]

        @pl.when(column != end)
        def _():
            to_block(way, band).wait_recv()

        @pl.when(column == end)
        def _():
            for index in range(len(COLUMNS)):
                from_column(way, band, index).wait_recv()

    def departed(way, band):
        start, end = BETWEEN[way], BETWEEN[1 - way]

        @pl.when(column != start)
        def _():
            to_block(way, band).wait_send()

        @pl.when(column == start)
        def _():
            for index in range(len(COLUMNS)):
                to_column(way, band, index).wait_send()

        @pl.when(relays & (column != end))
        def _():
            from_column(way, band, 0).wait_send()

    def put_packed(ref, band, x, plane):
        start = pl.multiple_of((band * SLAB + x) * ROWS, 8)
        for k, part in enumerate(pack(plane)):
            ref[pl.ds(start + 24 * k, 24), :] = part

    def get_packed(ref, band, x):
        start = pl.multiple_of((band * SLAB + x) * ROWS, 8)
        return unpack([ref[pl.ds(start + 24 * k, 24), :] for k in range(3)])

    for band in range(2):

        @pl.loop(0, SLAB)
        def _(x):
            plane = own_ref[band, x]
            bands[band, x] = plane
            put_packed(band_out, band, x, plane)

    pl.semaphore_wait(barrier, peers)
    for band in range(2):
        depart(0, band)

    acc[...] = jnp.zeros_like(acc)

    def pair(field):
        first = jnp.where(field < 3, field // 2, (field + 1) % 2)
        second = jnp.where(field < 3, (field + 1) // 2, 2 + (field - 3) // 2)
        return first, second

    def forward(field):
        first, second = pair(field)
        for group in range(0, SLAB, 4):
            density = bands[first, pl.ds(group, 4)] * bands[second, pl.ds(group, 4)]
            along_z = from_right(density.reshape(4 * NG, NG), right_ref)
            for i in range(4):
                plane = from_left(plane_ref[...], along_z[i * NG : (i + 1) * NG])
                parts = pack(plane)
                base = field * (GRID * MSG) + group + i
                for t in range(8):
                    tile = parts[t // 3][t % 3 * 8 : t % 3 * 8 + 8]
                    sent[pl.ds(base + t * SLAB, GRID, stride=MSG), :] = tile
                for t in (8, 9):
                    tile = parts[2][4 * t - 16 : 4 * t - 12]
                    sent[pl.ds(base + MSG + t * SLAB, GRID // 2, stride=2 * MSG), :] = tile

    def make_coulomb():
        factor = 4.0 * np.pi / (2.0 * np.pi / BOX_EDGE) ** 2 / float(NG) ** 3

        def square(index):
            folded = jnp.minimum(index, NG - index)
            return folded * folded

        kx = lax.broadcasted_iota(jnp.int32, (NG, 128), 0)
        lane = lax.broadcasted_iota(jnp.int32, (NG, 128), 1)

        @pl.loop(0, SHARE[1])
        def _(t):
            row = jnp.where(t < 8, t * GRID + me, 32 + 4 * t + me // 2)
            part, a = row // 24, row % 24
            ky = jnp.where(lane < NG, 24 * part + a, 72 + a)
            kz = jnp.where(lane < NG, lane, 32 * part + lane - NG)
            total = square(kx) + square(ky) + square(kz)
            safe = jnp.maximum(total, 1).astype(F32)
            coulomb[t] = jnp.where(total > 0, factor / safe, 0.0)

    def solve(field):
        await_all(field, 0)
        base = field * (GRID * MSG)

        def solve_tile(t):
            rows = jnp.concatenate(
                [got[pl.ds(base + t * SLAB + x, GRID, stride=MSG), :] for x in range(SLAB)],
                axis=0,
            )
            spectrum = from_left(there_ref[...], rows) * coulomb[t]
            mixed = from_left(back_ref[...], spectrum)
            for x in range(SLAB):
                ret_sent[pl.ds(base + t * SLAB + x, GRID, stride=MSG), :] = mixed[
                    x * GRID : (x + 1) * GRID
                ]

        for t in range(SHARE[0]):
            solve_tile(t)

        @pl.when(me % 2 == 1)
        def _():
            for t in range(SHARE[0], SHARE[1]):
                solve_tile(t)

        send_all(field, 1)

    def backward(field):
        await_all(field, 1)
        first, second = pair(field)
        base = field * (GRID * MSG)
        for group in range(0, SLAB, 4):
            planes = []
            for i in range(4):
                tiles = [
                    ret_got[pl.ds(base + t * SLAB + group + i, GRID, stride=MSG), :]
                    for t in range(8)
                ]
                start = base + MSG + group + i
                halves = [
                    ret_got[pl.ds(start + t * SLAB, GRID // 2, stride=2 * MSG), :]
                    for t in (8, 9)
                ]
                tiles.append(jnp.concatenate(halves, axis=0))
                parts = [jnp.concatenate(tiles[3 * k : 3 * k + 3], axis=0) for k in range(3)]
                planes.append(from_left(plane_ref[...], unpack(parts)))
            potential = from_right(jnp.concatenate(planes, axis=0), right_ref)
            potential = potential.reshape(4, NG, NG)
            here = pl.ds(group, 4)
            acc[first, here] += potential * bands[second, here]

            @pl.when(first != second)
            def _():
                acc[second, here] += potential * bands[first, here]

    def give_back(band):
        @pl.loop(0, SLAB)
        def _(x):
            put_packed(theirs_out, band, x, acc[2 + band, x])

        depart(1, band)

    def at(step, fields):
        return sum(jnp.where(step == i, field, 0) for i, field in enumerate(fields))

    @pl.loop(0, len(FORWARD))
    def _(step):
        @pl.when(step == 3)
        def _():
            for band in range(2):
                arrive(0, band)

                @pl.loop(0, SLAB)
                def _(x):
                    bands[2 + band, x] = get_packed(band_in, band, x)

        forward_field = at(step, FORWARD)

        @pl.when(forward_field >= 0)
        def _():
            forward(forward_field)

        @pl.when(step == 1)
        def _():
            for band in range(2):
                relay_in(0, band)

        @pl.when(forward_field >= 0)
        def _():
            send_all(forward_field, 0)

        @pl.when(step == 2)
        def _():
            make_coulomb()

        solve_field = at(step, SOLVE)
        backward_field = at(step, BACKWARD)

        @pl.when((solve_field >= 0) & (step < 12))
        def _():
            solve(solve_field)

        @pl.when(backward_field >= 0)
        def _():
            backward(backward_field)

        @pl.when(step == 10)
        def _():
            give_back(0)

        @pl.when(step == 12)
        def _():
            give_back(1)
            relay_in(1, 0)

        @pl.when(step == 13)
        def _():
            relay_in(1, 1)

        @pl.when((solve_field >= 0) & (step >= 12))
        def _():
            solve(solve_field)

    for band in range(2):
        arrive(1, band)

        @pl.loop(0, SLAB)
        def _(x):
            out_ref[band, x] = -(acc[band, x] + get_packed(theirs_in, band, x))

    @pl.loop(0, FIELDS)
    def _(field):
        for way in range(2):
            await_sent(field, way)

    for band in range(2):
        for way in range(2):
            departed(way, band)


def body(blocks, bands):
    count, slab, plane = bands.shape
    own = bands.reshape(count, slab, NG, NG)
    constants = [jnp.asarray(table) for table in tables()]
    vmem = pl.BlockSpec(memory_space=pltpu.VMEM)
    messages = pltpu.VMEM((FIELDS * GRID * MSG, 128), F32)
    packed = pltpu.VMEM((count * SLAB * ROWS, 128), F32)
    stops = pltpu.VMEM((2 * count * (SLAB // len(COLUMNS)) * ROWS, 128), F32)
    out = pl.pallas_call(
        functools.partial(kernel, blocks),
        out_shape=jax.ShapeDtypeStruct((count, slab, NG, NG), F32),
        in_specs=[vmem] * 5,
        out_specs=vmem,
        scratch_shapes=[
            pltpu.VMEM((2 * count, SLAB, NG, NG), F32),
            pltpu.VMEM((2 * count, SLAB, NG, NG), F32),
            pltpu.VMEM((SHARE[1], NG, 128), F32),
            messages,
            messages,
            messages,
            messages,
            packed,
            packed,
            packed,
            packed,
            pltpu.SemaphoreType.DMA((FIELDS, GRID)),
            pltpu.SemaphoreType.DMA((FIELDS, GRID)),
            pltpu.SemaphoreType.DMA((FIELDS, GRID)),
            pltpu.SemaphoreType.DMA((FIELDS, GRID)),
            pltpu.SemaphoreType.DMA((2, FIELDS)),
            pltpu.SemaphoreType.DMA((2, 2)),
            pltpu.SemaphoreType.DMA((2, 2)),
            stops,
            pltpu.SemaphoreType.DMA((2, 2, len(COLUMNS))),
            pltpu.SemaphoreType.DMA((2, 2)),
            pltpu.SemaphoreType.DMA((2, 2)),
            pltpu.SemaphoreType.DMA((2, 2, len(COLUMNS))),
        ],
        compiler_params=pltpu.CompilerParams(
            collective_id=0, has_side_effects=True, vmem_limit_bytes=48 * 1024 * 1024
        ),
    )(own, *constants)
    return out.reshape(count, slab, plane)


def solution(mesh):
    spec = P("blk", "grid", None)
    return jax.shard_map(
        functools.partial(body, mesh.shape["blk"]),
        mesh=mesh,
        in_specs=(spec,),
        out_specs=spec,
        check_vma=False,
    )
```

```python
import functools

import jax
import jax.numpy as jnp
import ml_dtypes
import numpy as np
from jax import lax
from jax.experimental import pallas as pl
from jax.experimental.pallas import tpu as pltpu
from jax.sharding import PartitionSpec as P

NG = 96
BOX_EDGE = 23.47
MESH = pl.DeviceIdType.MESH
F32 = jnp.float32
BF16 = jnp.bfloat16

GRID = 8
SLAB = NG // GRID
ROWS = NG * NG // 128
SHARE = 8, 10
MSG = SHARE[1] * SLAB
FIELDS = 7

LAYER = 16
COLUMNS = (0, 1, 2, 3, 4, 7, 8, 11, 12, 13, 14, 15)
BETWEEN = LAYER - 1, 0

FORWARD = (0, 1, 2, 3, 4, 5, 6, -1, -1, -1, -1, -1, -1, -1, -1, -1)
SOLVE = (-1, -1, -1, -1, -1, -1, -1, 3, 4, 5, 6, 0, 1, 2, -1, -1)
BACKWARD = (-1, -1, -1, -1, -1, -1, -1, -1, -1, 3, 4, 5, 6, 0, 1, 2)


def hartley(rows, cols):
    angle = (rows[:, None] * cols[None, :] % NG) * (2.0 * np.pi / NG)
    return np.cos(angle) + np.sin(angle)


def split_table(table):
    parts = []
    for _ in range(3):
        part = table.astype(np.float32).astype(ml_dtypes.bfloat16)
        parts.append(part)
        table = table - part.astype(np.float64)
    return parts


def left_table(table):
    return np.concatenate([np.concatenate([part, part], axis=1) for part in split_table(table)])


def right_table(table):
    parts = [np.pad(part, ((0, 0), (0, 128 - NG))) for part in split_table(table)]
    return np.concatenate(parts, axis=1)


def tables():
    plain = np.arange(NG)
    mixed = np.arange(NG) % GRID * SLAB + np.arange(NG) // GRID
    return (
        right_table(hartley(plain, plain)),
        left_table(hartley(plain, plain)),
        left_table(hartley(plain, mixed)),
        left_table(hartley(mixed, plain)),
    )


def split(value):
    high = value.astype(BF16)
    low = (value - high.astype(F32)).astype(BF16)
    return high, low


def dot(a, b):
    return jnp.dot(a, b, preferred_element_type=F32)


def from_left(table, value):
    high, low = split(value)
    both = dot(table, jnp.concatenate([high, low], axis=0))
    return both[:NG] + (both[NG : 2 * NG] + both[2 * NG :])


def from_right(value, right_ref):
    high, low = split(value)
    above = dot(high, right_ref[:, :256])
    below = dot(low, right_ref[:, :256])
    rest = dot(high, right_ref[:, 256:])
    second = above[:, 128 : 128 + NG] + below[:, :NG]
    return above[:, :NG] + (second + (below[:, 128 : 128 + NG] + rest[:, :NG]))


def pack(plane):
    last = plane[72:96]
    return [
        jnp.concatenate([plane[24 * k : 24 * k + 24], last[:, 32 * k : 32 * k + 32]], axis=1)
        for k in range(3)
    ]


def unpack(parts):
    last = jnp.concatenate([part[:, 96:128] for part in parts], axis=1)
    return jnp.concatenate([part[:, :96] for part in parts] + [last], axis=0)


def kernel(
    blocks,
    own_ref,
    right_ref,
    plane_ref,
    there_ref,
    back_ref,
    out_ref,
    bands,
    acc,
    coulomb,
    sent,
    got,
    ret_sent,
    ret_got,
    band_out,
    band_in,
    theirs_out,
    theirs_in,
    fwd_send,
    fwd_recv,
    bwd_send,
    bwd_recv,
    self_sem,
    blk_send,
    blk_recv,
    stop,
    first_send,
    stop_recv,
    second_send,
    last_recv,
):
    blk = lax.axis_index("blk")
    me = lax.axis_index("grid")
    after = lax.rem(blk + 1, blocks)
    before = lax.rem(blk + blocks - 1, blocks)

    column = lax.rem(blk, LAYER)
    layer = blk - column
    piece = sum(jnp.where(column == c, i, 0) for i, c in enumerate(COLUMNS))
    relays = functools.reduce(jnp.logical_or, [column == c for c in COLUMNS])

    barrier = pltpu.get_barrier_semaphore()

    def greet(other):
        pl.semaphore_signal(barrier, inc=1, device_id=other, device_id_type=MESH)

    for d in range(1, GRID):
        greet((blk, lax.rem(me + d, GRID)))

    at_end = (column == 0) | (column == LAYER - 1)
    peers = GRID - 1 + jnp.where(relays, jnp.where(at_end, len(COLUMNS) + 1, 2), 0)
    for c in range(LAYER):
        linked = (column == c - 1) | (column == c + 1)
        if c in COLUMNS:
            linked = linked | ((relays if c in BETWEEN else at_end) & (column != c))
        peers = peers + jnp.where(linked, 1, 0)

        @pl.when(linked)
        def _():
            greet((layer + c, me))

    def other_layer(way):
        return lax.rem(layer + (LAYER if way == 0 else blocks - LAYER), blocks)

    for way, end in enumerate(BETWEEN):

        @pl.when(column == end)
        def _():
            for c in COLUMNS:
                greet((other_layer(way) + c, me))

        @pl.when(relays & (column != BETWEEN[1 - way]))
        def _():
            greet((other_layer(1 - way) + end, me))

    def message(field, device, share):
        return pl.ds(pl.multiple_of((field * GRID + device) * MSG, 8), share * SLAB)

    def exchange(source, target, send_sem, recv_sem, field, peer, share):
        return pltpu.make_async_remote_copy(
            src_ref=source.at[message(field, peer, share)],
            dst_ref=target.at[message(field, me, share)],
            send_sem=send_sem.at[field, peer],
            recv_sem=recv_sem.at[field, me],
            device_id=(blk, peer),
            device_id_type=MESH,
        )

    def arrival(source, target, send_sem, recv_sem, field, peer, share):
        return pltpu.make_async_remote_copy(
            src_ref=source.at[message(field, peer, share)],
            dst_ref=target.at[message(field, peer, share)],
            send_sem=send_sem.at[field, peer],
            recv_sem=recv_sem.at[field, peer],
            device_id=(blk, peer),
            device_id_type=MESH,
        )

    def keep(source, target, field, way, share):
        here = message(field, me, share)
        return pltpu.make_async_copy(source.at[here], target.at[here], self_sem.at[way, field])

    buffers = ((sent, got, fwd_send, fwd_recv), (ret_sent, ret_got, bwd_send, bwd_recv))

    def by_parity(run):
        for parity in range(2):

            @pl.when(me % 2 == parity)
            def _():
                run(parity)

    def send_all(field, way):
        def run(parity):
            for d in (4, 3, 5, 2, 6, 1, 7):
                share = SHARE[parity if way else (parity + d) % 2]
                exchange(*buffers[way], field, lax.rem(me + d, GRID), share).start()
            keep(*buffers[way][:2], field, way, SHARE[parity]).start()

        by_parity(run)

    def await_all(field, way):
        def run(parity):
            keep(*buffers[way][:2], field, way, SHARE[parity]).wait()
            for d in range(1, GRID):
                share = SHARE[(parity + d) % 2 if way else parity]
                arrival(*buffers[way], field, lax.rem(me + d, GRID), share).wait_recv()

        by_parity(run)

    def await_sent(field, way):
        def run(parity):
            for d in range(1, GRID):
                share = SHARE[parity if way else (parity + d) % 2]
                exchange(*buffers[way], field, lax.rem(me + d, GRID), share).wait_send()

        by_parity(run)

    def band_rows(band):
        return pl.ds(pl.multiple_of(band * (SLAB * ROWS), 8), SLAB * ROWS)

    travel = ((band_out, band_in), (theirs_out, theirs_in))
    planes = SLAB // len(COLUMNS)

    def piece_rows(band, index):
        return pl.ds(pl.multiple_of((band * SLAB + index * planes) * ROWS, 8), planes * ROWS)

    def stop_rows(way, band):
        return pl.ds((way * 2 + band) * planes * ROWS, planes * ROWS)

    def to_block(way, band):
        source, target = travel[way]
        return pltpu.make_async_remote_copy(
            src_ref=source.at[band_rows(band)],
            dst_ref=target.at[band_rows(band)],
            send_sem=blk_send.at[way, band],
            recv_sem=blk_recv.at[way, band],
            device_id=((after, before)[way], me),
            device_id_type=MESH,
        )

    def to_column(way, band, index):
        if COLUMNS[index] == BETWEEN[way]:
            target = travel[way][1].at[piece_rows(band, index)]
            done = last_recv.at[way, band, index]
            place = other_layer(way) + BETWEEN[1 - way]
        else:
            target, done = stop.at[stop_rows(way, band)], stop_recv.at[way, band]
            place = layer + COLUMNS[index]
        return pltpu.make_async_remote_copy(
            src_ref=travel[way][0].at[piece_rows(band, index)],
            dst_ref=target,
            send_sem=first_send.at[way, band, index],
            recv_sem=done,
            device_id=(place, me),
            device_id_type=MESH,
        )

    def from_column(way, band, index):
        return pltpu.make_async_remote_copy(
            src_ref=stop.at[stop_rows(way, band)],
            dst_ref=travel[way][1].at[piece_rows(band, index)],
            send_sem=second_send.at[way, band],
            recv_sem=last_recv.at[way, band, index],
            device_id=(other_layer(way) + BETWEEN[1 - way], me),
            device_id_type=MESH,
        )

    def depart(way, band):
        start = BETWEEN[way]

        @pl.when(column != start)
        def _():
            to_block(way, band).start()

        @pl.when(column == start)
        def _():
            for index in range(len(COLUMNS)):
                to_column(way, band, index).start()

    def relay_in(way, band):
        @pl.when(relays & (column != BETWEEN[way]))
        def _():
            to_column(way, band, COLUMNS.index(BETWEEN[1 - way])).wait_recv()
            from_column(way, band, piece).start()

    def arrive(way, band):
        end = BETWEEN[1 - way]

        @pl.when(column != end)
        def _():
            to_block(way, band).wait_recv()

        @pl.when(column == end)
        def _():
            for index in range(len(COLUMNS)):
                from_column(way, band, index).wait_recv()

    def departed(way, band):
        start = BETWEEN[way]

        @pl.when(column != start)
        def _():
            to_block(way, band).wait_send()

        @pl.when(column == start)
        def _():
            for index in range(len(COLUMNS)):
                to_column(way, band, index).wait_send()

        @pl.when(relays & (column != start))
        def _():
            from_column(way, band, 0).wait_send()

    def put_packed(ref, band, x, plane):
        start = pl.multiple_of((band * SLAB + x) * ROWS, 8)
        for k, part in enumerate(pack(plane)):
            ref[pl.ds(start + 24 * k, 24), :] = part

    def get_packed(ref, band, x):
        start = pl.multiple_of((band * SLAB + x) * ROWS, 8)
        return unpack([ref[pl.ds(start + 24 * k, 24), :] for k in range(3)])

    for band in range(2):

        @pl.loop(0, SLAB)
        def _(x):
            plane = own_ref[band, x]
            bands[band, x] = plane
            put_packed(band_out, band, x, plane)

    pl.semaphore_wait(barrier, peers)
    for band in range(2):
        depart(0, band)

    acc[...] = jnp.zeros_like(acc)

    def pair(field):
        first = jnp.where(field < 3, field // 2, (field + 1) % 2)
        second = jnp.where(field < 3, (field + 1) // 2, 2 + (field - 3) // 2)
        return first, second

    def forward(field):
        first, second = pair(field)
        for group in range(0, SLAB, 4):
            density = bands[first, pl.ds(group, 4)] * bands[second, pl.ds(group, 4)]
            along_z = from_right(density.reshape(4 * NG, NG), right_ref)
            for i in range(4):
                plane = from_left(plane_ref[...], along_z[i * NG : (i + 1) * NG])
                parts = pack(plane)
                base = field * (GRID * MSG) + group + i
                for t in range(8):
                    tile = parts[t // 3][t % 3 * 8 : t % 3 * 8 + 8]
                    sent[pl.ds(base + t * SLAB, GRID, stride=MSG), :] = tile
                for t in (8, 9):
                    tile = parts[2][4 * t - 16 : 4 * t - 12]
                    sent[pl.ds(base + MSG + t * SLAB, GRID // 2, stride=2 * MSG), :] = tile

    def make_coulomb():
        factor = 4.0 * np.pi / (2.0 * np.pi / BOX_EDGE) ** 2 / float(NG) ** 3

        def square(index):
            folded = jnp.minimum(index, NG - index)
            return folded * folded

        kx = lax.broadcasted_iota(jnp.int32, (NG, 128), 0)
        lane = lax.broadcasted_iota(jnp.int32, (NG, 128), 1)

        @pl.loop(0, SHARE[1])
        def _(t):
            row = jnp.where(t < 8, t * GRID + me, 32 + 4 * t + me // 2)
            part, a = row // 24, row % 24
            ky = jnp.where(lane < NG, 24 * part + a, 72 + a)
            kz = jnp.where(lane < NG, lane, 32 * part + lane - NG)
            total = square(kx) + square(ky) + square(kz)
            safe = jnp.maximum(total, 1).astype(F32)
            coulomb[t] = jnp.where(total > 0, factor / safe, 0.0)

    def solve(field):
        await_all(field, 0)
        base = field * (GRID * MSG)

        def solve_tile(t):
            rows = jnp.concatenate(
                [got[pl.ds(base + t * SLAB + x, GRID, stride=MSG), :] for x in range(SLAB)],
                axis=0,
            )
            spectrum = from_left(there_ref[...], rows) * coulomb[t]
            mixed = from_left(back_ref[...], spectrum)
            for x in range(SLAB):
                ret_sent[pl.ds(base + t * SLAB + x, GRID, stride=MSG), :] = mixed[
                    x * GRID : (x + 1) * GRID
                ]

        for t in range(SHARE[0]):
            solve_tile(t)

        @pl.when(me % 2 == 1)
        def _():
            for t in range(SHARE[0], SHARE[1]):
                solve_tile(t)

        send_all(field, 1)

    def backward(field):
        await_all(field, 1)
        first, second = pair(field)
        base = field * (GRID * MSG)
        for group in range(0, SLAB, 4):
            planes = []
            for i in range(4):
                tiles = [
                    ret_got[pl.ds(base + t * SLAB + group + i, GRID, stride=MSG), :]
                    for t in range(8)
                ]
                start = base + MSG + group + i
                halves = [
                    ret_got[pl.ds(start + t * SLAB, GRID // 2, stride=2 * MSG), :]
                    for t in (8, 9)
                ]
                tiles.append(jnp.concatenate(halves, axis=0))
                parts = [jnp.concatenate(tiles[3 * k : 3 * k + 3], axis=0) for k in range(3)]
                planes.append(from_left(plane_ref[...], unpack(parts)))
            potential = from_right(jnp.concatenate(planes, axis=0), right_ref)
            potential = potential.reshape(4, NG, NG)
            here = pl.ds(group, 4)
            acc[first, here] += potential * bands[second, here]

            @pl.when(first != second)
            def _():
                acc[second, here] += potential * bands[first, here]

    def give_back(band):
        @pl.loop(0, SLAB)
        def _(x):
            put_packed(theirs_out, band, x, acc[2 + band, x])

        depart(1, band)

    def at(step, fields):
        return sum(jnp.where(step == i, field, 0) for i, field in enumerate(fields))

    @pl.loop(0, len(FORWARD))
    def _(step):
        @pl.when(step == 3)
        def _():
            for band in range(2):
                arrive(0, band)

                @pl.loop(0, SLAB)
                def _(x):
                    bands[2 + band, x] = get_packed(band_in, band, x)

        forward_field = at(step, FORWARD)

        @pl.when(forward_field >= 0)
        def _():
            forward(forward_field)

        @pl.when(step == 1)
        def _():
            for band in range(2):
                relay_in(0, band)

        @pl.when(forward_field >= 0)
        def _():
            send_all(forward_field, 0)

        @pl.when(step == 2)
        def _():
            make_coulomb()

        solve_field = at(step, SOLVE)
        backward_field = at(step, BACKWARD)

        @pl.when((solve_field >= 0) & (step < 12))
        def _():
            solve(solve_field)

        @pl.when(backward_field >= 0)
        def _():
            backward(backward_field)

        @pl.when(step == 10)
        def _():
            give_back(0)

        @pl.when(step == 12)
        def _():
            give_back(1)
            relay_in(1, 0)

        @pl.when(step == 13)
        def _():
            relay_in(1, 1)

        @pl.when((solve_field >= 0) & (step >= 12))
        def _():
            solve(solve_field)

    for band in range(2):
        arrive(1, band)

        @pl.loop(0, SLAB)
        def _(x):
            out_ref[band, x] = -(acc[band, x] + get_packed(theirs_in, band, x))

    @pl.loop(0, FIELDS)
    def _(field):
        for way in range(2):
            await_sent(field, way)

    for band in range(2):
        for way in range(2):
            departed(way, band)


def body(blocks, bands):
    count, slab, plane = bands.shape
    own = bands.reshape(count, slab, NG, NG)
    constants = [jnp.asarray(table) for table in tables()]
    vmem = pl.BlockSpec(memory_space=pltpu.VMEM)
    messages = pltpu.VMEM((FIELDS * GRID * MSG, 128), F32)
    packed = pltpu.VMEM((count * SLAB * ROWS, 128), F32)
    stops = pltpu.VMEM((2 * count * (SLAB // len(COLUMNS)) * ROWS, 128), F32)
    out = pl.pallas_call(
        functools.partial(kernel, blocks),
        out_shape=jax.ShapeDtypeStruct((count, slab, NG, NG), F32),
        in_specs=[vmem] * 5,
        out_specs=vmem,
        scratch_shapes=[
            pltpu.VMEM((2 * count, SLAB, NG, NG), F32),
            pltpu.VMEM((2 * count, SLAB, NG, NG), F32),
            pltpu.VMEM((SHARE[1], NG, 128), F32),
            messages,
            messages,
            messages,
            messages,
            packed,
            packed,
            packed,
            packed,
            pltpu.SemaphoreType.DMA((FIELDS, GRID)),
            pltpu.SemaphoreType.DMA((FIELDS, GRID)),
            pltpu.SemaphoreType.DMA((FIELDS, GRID)),
            pltpu.SemaphoreType.DMA((FIELDS, GRID)),
            pltpu.SemaphoreType.DMA((2, FIELDS)),
            pltpu.SemaphoreType.DMA((2, 2)),
            pltpu.SemaphoreType.DMA((2, 2)),
            stops,
            pltpu.SemaphoreType.DMA((2, 2, len(COLUMNS))),
            pltpu.SemaphoreType.DMA((2, 2)),
            pltpu.SemaphoreType.DMA((2, 2)),
            pltpu.SemaphoreType.DMA((2, 2, len(COLUMNS))),
        ],
        compiler_params=pltpu.CompilerParams(
            collective_id=0, has_side_effects=True, vmem_limit_bytes=48 * 1024 * 1024
        ),
    )(own, *constants)
    return out.reshape(count, slab, plane)


def solution(mesh):
    spec = P("blk", "grid", None)
    return jax.shard_map(
        functools.partial(body, mesh.shape["blk"]),
        mesh=mesh,
        in_specs=(spec,),
        out_specs=spec,
        check_vma=False,
    )
```

```python
import functools

import jax
import jax.numpy as jnp
import ml_dtypes
import numpy as np
from jax import lax
from jax.experimental import pallas as pl
from jax.experimental.pallas import tpu as pltpu
from jax.sharding import PartitionSpec as P

NG = 96
BOX_EDGE = 23.47
MESH = pl.DeviceIdType.MESH
F32 = jnp.float32
BF16 = jnp.bfloat16

GRID = 8
SLAB = NG // GRID
ROWS = NG * NG // 128
SHARE = 8, 10
MSG = SHARE[1] * SLAB
FIELDS = 7

LAYER = 16
COLUMNS = (0, 1, 2, 3, 4, 7, 8, 11, 12, 13, 14, 15)
BETWEEN = LAYER - 1, 0

FORWARD = (0, 1, 2, 3, 4, 5, 6, -1, -1, -1, -1, -1, -1, -1, -1, -1)
SOLVE = (-1, -1, -1, -1, -1, -1, -1, 3, 4, 5, 6, 0, 1, 2, -1, -1)
BACKWARD = (-1, -1, -1, -1, -1, -1, -1, -1, -1, 3, 4, 5, 6, 0, 1, 2)


def hartley(rows, cols):
    angle = (rows[:, None] * cols[None, :] % NG) * (2.0 * np.pi / NG)
    return np.cos(angle) + np.sin(angle)


def split_table(table):
    parts = []
    for _ in range(3):
        part = table.astype(np.float32).astype(ml_dtypes.bfloat16)
        parts.append(part)
        table = table - part.astype(np.float64)
    return parts


def left_table(table):
    return np.concatenate([np.concatenate([part, part], axis=1) for part in split_table(table)])


def right_table(table):
    parts = [np.pad(part, ((0, 0), (0, 128 - NG))) for part in split_table(table)]
    return np.concatenate(parts, axis=1)


def tables():
    plain = np.arange(NG)
    mixed = np.arange(NG) % GRID * SLAB + np.arange(NG) // GRID
    return (
        right_table(hartley(plain, plain)),
        left_table(hartley(plain, plain)),
        left_table(hartley(plain, mixed)),
        left_table(hartley(mixed, plain)),
    )


def split(value):
    high = value.astype(BF16)
    low = (value - high.astype(F32)).astype(BF16)
    return high, low


def dot(a, b):
    return jnp.dot(a, b, preferred_element_type=F32)


def from_left(table, value):
    high, low = split(value)
    both = dot(table, jnp.concatenate([high, low], axis=0))
    return both[:NG] + (both[NG : 2 * NG] + both[2 * NG :])


def from_right(value, right_ref):
    high, low = split(value)
    above = dot(high, right_ref[:, :256])
    below = dot(low, right_ref[:, :256])
    rest = dot(high, right_ref[:, 256:])
    second = above[:, 128 : 128 + NG] + below[:, :NG]
    return above[:, :NG] + (second + (below[:, 128 : 128 + NG] + rest[:, :NG]))


def pack(plane):
    last = plane[72:96]
    return [
        jnp.concatenate([plane[24 * k : 24 * k + 24], last[:, 32 * k : 32 * k + 32]], axis=1)
        for k in range(3)
    ]


def unpack(parts):
    last = jnp.concatenate([part[:, 96:128] for part in parts], axis=1)
    return jnp.concatenate([part[:, :96] for part in parts] + [last], axis=0)


def kernel(
    blocks,
    own_ref,
    right_ref,
    plane_ref,
    there_ref,
    back_ref,
    out_ref,
    bands,
    acc,
    coulomb,
    sent,
    got,
    ret_sent,
    ret_got,
    band_out,
    band_in,
    theirs_out,
    theirs_in,
    fwd_send,
    fwd_recv,
    bwd_send,
    bwd_recv,
    self_sem,
    blk_send,
    blk_recv,
    stop,
    first_send,
    stop_recv,
    second_send,
    last_recv,
):
    blk = lax.axis_index("blk")
    me = lax.axis_index("grid")
    after = lax.rem(blk + 1, blocks)
    before = lax.rem(blk + blocks - 1, blocks)

    column = lax.rem(blk, LAYER)
    layer = blk - column
    piece = sum(jnp.where(column == c, i, 0) for i, c in enumerate(COLUMNS))
    relays = functools.reduce(jnp.logical_or, [column == c for c in COLUMNS])

    barrier = pltpu.get_barrier_semaphore()

    def greet(other):
        pl.semaphore_signal(barrier, inc=1, device_id=other, device_id_type=MESH)

    for d in range(1, GRID):
        greet((blk, lax.rem(me + d, GRID)))

    at_end = (column == 0) | (column == LAYER - 1)
    peers = GRID - 1 + jnp.where(relays, jnp.where(at_end, len(COLUMNS) + 1, 2), 0)
    for c in range(LAYER):
        linked = (column == c - 1) | (column == c + 1)
        if c in COLUMNS:
            linked = linked | ((relays if c in BETWEEN else at_end) & (column != c))
        peers = peers + jnp.where(linked, 1, 0)

        @pl.when(linked)
        def _():
            greet((layer + c, me))

    def other_layer(way):
        return lax.rem(layer + (LAYER if way == 0 else blocks - LAYER), blocks)

    for way, end in enumerate(BETWEEN):

        @pl.when(column == end)
        def _():
            for c in COLUMNS:
                greet((other_layer(way) + c, me))

        @pl.when(relays & (column != BETWEEN[1 - way]))
        def _():
            greet((other_layer(1 - way) + end, me))

    def message(field, device, share):
        return pl.ds(pl.multiple_of((field * GRID + device) * MSG, 8), share * SLAB)

    def exchange(source, target, send_sem, recv_sem, field, peer, share):
        return pltpu.make_async_remote_copy(
            src_ref=source.at[message(field, peer, share)],
            dst_ref=target.at[message(field, me, share)],
            send_sem=send_sem.at[field, peer],
            recv_sem=recv_sem.at[field, me],
            device_id=(blk, peer),
            device_id_type=MESH,
        )

    def arrival(source, target, send_sem, recv_sem, field, peer, share):
        return pltpu.make_async_remote_copy(
            src_ref=source.at[message(field, peer, share)],
            dst_ref=target.at[message(field, peer, share)],
            send_sem=send_sem.at[field, peer],
            recv_sem=recv_sem.at[field, peer],
            device_id=(blk, peer),
            device_id_type=MESH,
        )

    def keep(source, target, field, way, share):
        here = message(field, me, share)
        return pltpu.make_async_copy(source.at[here], target.at[here], self_sem.at[way, field])

    buffers = ((sent, got, fwd_send, fwd_recv), (ret_sent, ret_got, bwd_send, bwd_recv))

    def by_parity(run):
        for parity in range(2):

            @pl.when(me % 2 == parity)
            def _():
                run(parity)

    def send_all(field, way):
        def run(parity):
            for d in (4, 3, 5, 2, 6, 1, 7):
                share = SHARE[parity if way else (parity + d) % 2]
                exchange(*buffers[way], field, lax.rem(me + d, GRID), share).start()
            keep(*buffers[way][:2], field, way, SHARE[parity]).start()

        by_parity(run)

    def await_all(field, way):
        def run(parity):
            keep(*buffers[way][:2], field, way, SHARE[parity]).wait()
            for d in range(1, GRID):
                share = SHARE[(parity + d) % 2 if way else parity]
                arrival(*buffers[way], field, lax.rem(me + d, GRID), share).wait_recv()

        by_parity(run)

    def await_sent(field, way):
        def run(parity):
            for d in range(1, GRID):
                share = SHARE[parity if way else (parity + d) % 2]
                exchange(*buffers[way], field, lax.rem(me + d, GRID), share).wait_send()

        by_parity(run)

    def band_rows(band):
        return pl.ds(pl.multiple_of(band * (SLAB * ROWS), 8), SLAB * ROWS)

    travel = ((band_out, band_in), (theirs_out, theirs_in))
    planes = SLAB // len(COLUMNS)

    def piece_rows(band, index):
        return pl.ds(pl.multiple_of((band * SLAB + index * planes) * ROWS, 8), planes * ROWS)

    def stop_rows(way, band):
        return pl.ds((way * 2 + band) * planes * ROWS, planes * ROWS)

    def to_block(way, band):
        source, target = travel[way]
        return pltpu.make_async_remote_copy(
            src_ref=source.at[band_rows(band)],
            dst_ref=target.at[band_rows(band)],
            send_sem=blk_send.at[way, band],
            recv_sem=blk_recv.at[way, band],
            device_id=((after, before)[way], me),
            device_id_type=MESH,
        )

    def to_column(way, band, index):
        if COLUMNS[index] == BETWEEN[way]:
            target = travel[way][1].at[piece_rows(band, index)]
            done = last_recv.at[way, band, index]
            place = other_layer(way) + BETWEEN[1 - way]
        else:
            target, done = stop.at[stop_rows(way, band)], stop_recv.at[way, band]
            place = layer + COLUMNS[index]
        return pltpu.make_async_remote_copy(
            src_ref=travel[way][0].at[piece_rows(band, index)],
            dst_ref=target,
            send_sem=first_send.at[way, band, index],
            recv_sem=done,
            device_id=(place, me),
            device_id_type=MESH,
        )

    def from_column(way, band, index):
        return pltpu.make_async_remote_copy(
            src_ref=stop.at[stop_rows(way, band)],
            dst_ref=travel[way][1].at[piece_rows(band, index)],
            send_sem=second_send.at[way, band],
            recv_sem=last_recv.at[way, band, index],
            device_id=(other_layer(way) + BETWEEN[1 - way], me),
            device_id_type=MESH,
        )

    def depart(way, band):
        start = BETWEEN[way]

        @pl.when(column != start)
        def _():
            to_block(way, band).start()

        @pl.when(column == start)
        def _():
            for index in range(len(COLUMNS)):
                to_column(way, band, index).start()

    def relay_in(way, band):
        @pl.when(relays & (column != BETWEEN[way]))
        def _():
            to_column(way, band, COLUMNS.index(BETWEEN[1 - way])).wait_recv()
            from_column(way, band, piece).start()

    def arrive(way, band):
        end = BETWEEN[1 - way]

        @pl.when(column != end)
        def _():
            to_block(way, band).wait_recv()

        @pl.when(column == end)
        def _():
            for index in range(len(COLUMNS)):
                from_column(way, band, index).wait_recv()

    def departed(way, band):
        start = BETWEEN[way]

        @pl.when(column != start)
        def _():
            to_block(way, band).wait_send()

        @pl.when(column == start)
        def _():
            for index in range(len(COLUMNS)):
                to_column(way, band, index).wait_send()

        @pl.when(relays & (column != start))
        def _():
            from_column(way, band, 0).wait_send()

    def put_packed(ref, band, x, plane):
        start = pl.multiple_of((band * SLAB + x) * ROWS, 8)
        for k, part in enumerate(pack(plane)):
            ref[pl.ds(start + 24 * k, 24), :] = part

    def get_packed(ref, band, x):
        start = pl.multiple_of((band * SLAB + x) * ROWS, 8)
        return unpack([ref[pl.ds(start + 24 * k, 24), :] for k in range(3)])

    for band in range(2):

        @pl.loop(0, SLAB)
        def _(x):
            plane = own_ref[band, x]
            bands[band, x] = plane
            put_packed(band_out, band, x, plane)

        if band == 0:
            pl.semaphore_wait(barrier, peers)
        depart(0, band)

    acc[...] = jnp.zeros_like(acc)

    def pair(field):
        first = jnp.where(field < 3, field // 2, (field + 1) % 2)
        second = jnp.where(field < 3, (field + 1) // 2, 2 + (field - 3) // 2)
        return first, second

    def forward(field):
        first, second = pair(field)
        for group in range(0, SLAB, 4):
            density = bands[first, pl.ds(group, 4)] * bands[second, pl.ds(group, 4)]
            along_z = from_right(density.reshape(4 * NG, NG), right_ref)
            for i in range(4):
                plane = from_left(plane_ref[...], along_z[i * NG : (i + 1) * NG])
                parts = pack(plane)
                base = field * (GRID * MSG) + group + i
                for t in range(8):
                    tile = parts[t // 3][t % 3 * 8 : t % 3 * 8 + 8]
                    sent[pl.ds(base + t * SLAB, GRID, stride=MSG), :] = tile
                for t in (8, 9):
                    tile = parts[2][4 * t - 16 : 4 * t - 12]
                    sent[pl.ds(base + MSG + t * SLAB, GRID // 2, stride=2 * MSG), :] = tile

    def make_coulomb():
        factor = 4.0 * np.pi / (2.0 * np.pi / BOX_EDGE) ** 2 / float(NG) ** 3

        def square(index):
            folded = jnp.minimum(index, NG - index)
            return folded * folded

        kx = lax.broadcasted_iota(jnp.int32, (NG, 128), 0)
        lane = lax.broadcasted_iota(jnp.int32, (NG, 128), 1)

        @pl.loop(0, SHARE[1])
        def _(t):
            row = jnp.where(t < 8, t * GRID + me, 32 + 4 * t + me // 2)
            part, a = row // 24, row % 24
            ky = jnp.where(lane < NG, 24 * part + a, 72 + a)
            kz = jnp.where(lane < NG, lane, 32 * part + lane - NG)
            total = square(kx) + square(ky) + square(kz)
            safe = jnp.maximum(total, 1).astype(F32)
            coulomb[t] = jnp.where(total > 0, factor / safe, 0.0)

    def solve(field):
        await_all(field, 0)
        base = field * (GRID * MSG)

        def solve_tile(t):
            rows = jnp.concatenate(
                [got[pl.ds(base + t * SLAB + x, GRID, stride=MSG), :] for x in range(SLAB)],
                axis=0,
            )
            spectrum = from_left(there_ref[...], rows) * coulomb[t]
            mixed = from_left(back_ref[...], spectrum)
            for x in range(SLAB):
                ret_sent[pl.ds(base + t * SLAB + x, GRID, stride=MSG), :] = mixed[
                    x * GRID : (x + 1) * GRID
                ]

        for t in range(SHARE[0]):
            solve_tile(t)

        @pl.when(me % 2 == 1)
        def _():
            for t in range(SHARE[0], SHARE[1]):
                solve_tile(t)

        send_all(field, 1)

    def backward(field):
        await_all(field, 1)
        first, second = pair(field)
        base = field * (GRID * MSG)
        for group in range(0, SLAB, 4):
            planes = []
            for i in range(4):
                tiles = [
                    ret_got[pl.ds(base + t * SLAB + group + i, GRID, stride=MSG), :]
                    for t in range(8)
                ]
                start = base + MSG + group + i
                halves = [
                    ret_got[pl.ds(start + t * SLAB, GRID // 2, stride=2 * MSG), :]
                    for t in (8, 9)
                ]
                tiles.append(jnp.concatenate(halves, axis=0))
                parts = [jnp.concatenate(tiles[3 * k : 3 * k + 3], axis=0) for k in range(3)]
                planes.append(from_left(plane_ref[...], unpack(parts)))
            potential = from_right(jnp.concatenate(planes, axis=0), right_ref)
            potential = potential.reshape(4, NG, NG)
            here = pl.ds(group, 4)
            acc[first, here] += potential * bands[second, here]

            @pl.when(first != second)
            def _():
                acc[second, here] += potential * bands[first, here]

    def give_back(band):
        @pl.loop(0, SLAB)
        def _(x):
            put_packed(theirs_out, band, x, acc[2 + band, x])

        depart(1, band)

    def at(step, fields):
        return sum(jnp.where(step == i, field, 0) for i, field in enumerate(fields))

    @pl.loop(0, len(FORWARD))
    def _(step):
        for band in range(2):

            @pl.when(step == 3 + 2 * band)
            def _():
                arrive(0, band)

                @pl.loop(0, SLAB)
                def _(x):
                    bands[2 + band, x] = get_packed(band_in, band, x)

        forward_field = at(step, FORWARD)

        @pl.when(forward_field >= 0)
        def _():
            forward(forward_field)

        for band in range(2):

            @pl.when(step == band)
            def _():
                relay_in(0, band)

        @pl.when(forward_field >= 0)
        def _():
            send_all(forward_field, 0)

        @pl.when(step == 2)
        def _():
            make_coulomb()

        solve_field = at(step, SOLVE)
        backward_field = at(step, BACKWARD)

        solve_late = (step == 10) | (step >= 12)

        @pl.when((solve_field >= 0) & ~solve_late)
        def _():
            solve(solve_field)

        @pl.when(step == 12)
        def _():
            relay_in(1, 0)

        @pl.when(backward_field >= 0)
        def _():
            backward(backward_field)

        @pl.when(step == 10)
        def _():
            give_back(0)

        @pl.when(step == 12)
        def _():
            give_back(1)

        @pl.when(step == 13)
        def _():
            relay_in(1, 1)

        @pl.when((solve_field >= 0) & solve_late)
        def _():
            solve(solve_field)

    for band in range(2):
        arrive(1, band)

        @pl.loop(0, SLAB)
        def _(x):
            out_ref[band, x] = -(acc[band, x] + get_packed(theirs_in, band, x))

    @pl.loop(0, FIELDS)
    def _(field):
        for way in range(2):
            await_sent(field, way)

    for band in range(2):
        for way in range(2):
            departed(way, band)


def body(blocks, bands):
    count, slab, plane = bands.shape
    own = bands.reshape(count, slab, NG, NG)
    constants = [jnp.asarray(table) for table in tables()]
    vmem = pl.BlockSpec(memory_space=pltpu.VMEM)
    messages = pltpu.VMEM((FIELDS * GRID * MSG, 128), F32)
    packed = pltpu.VMEM((count * SLAB * ROWS, 128), F32)
    stops = pltpu.VMEM((2 * count * (SLAB // len(COLUMNS)) * ROWS, 128), F32)
    out = pl.pallas_call(
        functools.partial(kernel, blocks),
        out_shape=jax.ShapeDtypeStruct((count, slab, NG, NG), F32),
        in_specs=[vmem] * 5,
        out_specs=vmem,
        scratch_shapes=[
            pltpu.VMEM((2 * count, SLAB, NG, NG), F32),
            pltpu.VMEM((2 * count, SLAB, NG, NG), F32),
            pltpu.VMEM((SHARE[1], NG, 128), F32),
            messages,
            messages,
            messages,
            messages,
            packed,
            packed,
            packed,
            packed,
            pltpu.SemaphoreType.DMA((FIELDS, GRID)),
            pltpu.SemaphoreType.DMA((FIELDS, GRID)),
            pltpu.SemaphoreType.DMA((FIELDS, GRID)),
            pltpu.SemaphoreType.DMA((FIELDS, GRID)),
            pltpu.SemaphoreType.DMA((2, FIELDS)),
            pltpu.SemaphoreType.DMA((2, 2)),
            pltpu.SemaphoreType.DMA((2, 2)),
            stops,
            pltpu.SemaphoreType.DMA((2, 2, len(COLUMNS))),
            pltpu.SemaphoreType.DMA((2, 2)),
            pltpu.SemaphoreType.DMA((2, 2)),
            pltpu.SemaphoreType.DMA((2, 2, len(COLUMNS))),
        ],
        compiler_params=pltpu.CompilerParams(
            collective_id=0, has_side_effects=True, vmem_limit_bytes=48 * 1024 * 1024
        ),
    )(own, *constants)
    return out.reshape(count, slab, plane)


def solution(mesh):
    spec = P("blk", "grid", None)
    return jax.shard_map(
        functools.partial(body, mesh.shape["blk"]),
        mesh=mesh,
        in_specs=(spec,),
        out_specs=spec,
        check_vma=False,
    )
```

```python
import functools

import jax
import jax.numpy as jnp
import ml_dtypes
import numpy as np
from jax import lax
from jax.experimental import pallas as pl
from jax.experimental.pallas import tpu as pltpu
from jax.sharding import PartitionSpec as P

NG = 96
BOX_EDGE = 23.47
MESH = pl.DeviceIdType.MESH
F32 = jnp.float32
BF16 = jnp.bfloat16

GRID = 8
SLAB = NG // GRID
ROWS = NG * NG // 128
SHARE = 8, 10
MSG = SHARE[1] * SLAB
FIELDS = 7

LAYER = 16
COLUMNS = (0, 1, 2, 3, 4, 7, 8, 11, 12, 13, 14, 15)
BETWEEN = LAYER - 1, 0

FORWARD = (0, 1, 2, 3, 4, 5, 6, -1, -1, -1, -1, -1, -1, -1, -1, -1)
SOLVE = (-1, -1, -1, -1, -1, -1, -1, 3, 4, 5, 6, 0, 1, 2, -1, -1)
SOLVE_FIRST = (-1, -1, -1, -1, -1, -1, -1, 3, 4, 5, 6, -1, 0, 1, 2, -1)
BACKWARD = (-1, -1, -1, -1, -1, -1, -1, -1, -1, 3, 4, 5, 6, 0, 1, 2)


def hartley(rows, cols):
    angle = (rows[:, None] * cols[None, :] % NG) * (2.0 * np.pi / NG)
    return np.cos(angle) + np.sin(angle)


def split_table(table):
    parts = []
    for _ in range(3):
        part = table.astype(np.float32).astype(ml_dtypes.bfloat16)
        parts.append(part)
        table = table - part.astype(np.float64)
    return parts


def left_table(table):
    return np.concatenate([np.concatenate([part, part], axis=1) for part in split_table(table)])


def right_table(table):
    parts = [np.pad(part, ((0, 0), (0, 128 - NG))) for part in split_table(table)]
    return np.concatenate(parts, axis=1)


def tables():
    plain = np.arange(NG)
    mixed = np.arange(NG) % GRID * SLAB + np.arange(NG) // GRID
    return (
        right_table(hartley(plain, plain)),
        left_table(hartley(plain, plain)),
        left_table(hartley(plain, mixed)),
        left_table(hartley(mixed, plain)),
    )


def split(value):
    high = value.astype(BF16)
    low = (value - high.astype(F32)).astype(BF16)
    return high, low


def dot(a, b):
    return jnp.dot(a, b, preferred_element_type=F32)


def from_left(table, value):
    high, low = split(value)
    both = dot(table, jnp.concatenate([high, low], axis=0))
    return both[:NG] + (both[NG : 2 * NG] + both[2 * NG :])


def from_right(value, right_ref):
    high, low = split(value)
    above = dot(high, right_ref[:, :256])
    below = dot(low, right_ref[:, :256])
    rest = dot(high, right_ref[:, 256:])
    second = above[:, 128 : 128 + NG] + below[:, :NG]
    return above[:, :NG] + (second + (below[:, 128 : 128 + NG] + rest[:, :NG]))


def pack(plane):
    last = plane[72:96]
    return [
        jnp.concatenate([plane[24 * k : 24 * k + 24], last[:, 32 * k : 32 * k + 32]], axis=1)
        for k in range(3)
    ]


def unpack(parts):
    last = jnp.concatenate([part[:, 96:128] for part in parts], axis=1)
    return jnp.concatenate([part[:, :96] for part in parts] + [last], axis=0)


def kernel(
    blocks,
    own_ref,
    right_ref,
    plane_ref,
    there_ref,
    back_ref,
    out_ref,
    bands,
    acc,
    coulomb,
    sent,
    got,
    ret_sent,
    ret_got,
    band_out,
    band_in,
    theirs_out,
    theirs_in,
    fwd_send,
    fwd_recv,
    bwd_send,
    bwd_recv,
    self_sem,
    blk_send,
    blk_recv,
    stop,
    first_send,
    stop_recv,
    second_send,
    last_recv,
):
    blk = lax.axis_index("blk")
    me = lax.axis_index("grid")
    after = lax.rem(blk + 1, blocks)
    before = lax.rem(blk + blocks - 1, blocks)

    column = lax.rem(blk, LAYER)
    layer = blk - column
    piece = sum(jnp.where(column == c, i, 0) for i, c in enumerate(COLUMNS))
    relays = functools.reduce(jnp.logical_or, [column == c for c in COLUMNS])

    barrier = pltpu.get_barrier_semaphore()

    def greet(other):
        pl.semaphore_signal(barrier, inc=1, device_id=other, device_id_type=MESH)

    for d in range(1, GRID):
        greet((blk, lax.rem(me + d, GRID)))

    at_end = (column == 0) | (column == LAYER - 1)
    peers = GRID - 1 + jnp.where(relays, jnp.where(at_end, len(COLUMNS) + 1, 2), 0)
    for c in range(LAYER):
        linked = (column == c - 1) | (column == c + 1)
        if c in COLUMNS:
            linked = linked | ((relays if c in BETWEEN else at_end) & (column != c))
        peers = peers + jnp.where(linked, 1, 0)

        @pl.when(linked)
        def _():
            greet((layer + c, me))

    def other_layer(way):
        return lax.rem(layer + (LAYER if way == 0 else blocks - LAYER), blocks)

    for way, end in enumerate(BETWEEN):

        @pl.when(column == end)
        def _():
            for c in COLUMNS:
                greet((other_layer(way) + c, me))

        @pl.when(relays & (column != BETWEEN[1 - way]))
        def _():
            greet((other_layer(1 - way) + end, me))

    def message(field, device, share):
        return pl.ds(pl.multiple_of((field * GRID + device) * MSG, 8), share * SLAB)

    def exchange(source, target, send_sem, recv_sem, field, peer, share):
        return pltpu.make_async_remote_copy(
            src_ref=source.at[message(field, peer, share)],
            dst_ref=target.at[message(field, me, share)],
            send_sem=send_sem.at[field, peer],
            recv_sem=recv_sem.at[field, me],
            device_id=(blk, peer),
            device_id_type=MESH,
        )

    def arrival(source, target, send_sem, recv_sem, field, peer, share):
        return pltpu.make_async_remote_copy(
            src_ref=source.at[message(field, peer, share)],
            dst_ref=target.at[message(field, peer, share)],
            send_sem=send_sem.at[field, peer],
            recv_sem=recv_sem.at[field, peer],
            device_id=(blk, peer),
            device_id_type=MESH,
        )

    def keep(source, target, field, way, share):
        here = message(field, me, share)
        return pltpu.make_async_copy(source.at[here], target.at[here], self_sem.at[way, field])

    buffers = ((sent, got, fwd_send, fwd_recv), (ret_sent, ret_got, bwd_send, bwd_recv))

    def by_parity(run):
        for parity in range(2):

            @pl.when(me % 2 == parity)
            def _():
                run(parity)

    def send_all(field, way):
        def run(parity):
            for d in (4, 3, 5, 2, 6, 1, 7):
                share = SHARE[parity if way else (parity + d) % 2]
                exchange(*buffers[way], field, lax.rem(me + d, GRID), share).start()
            keep(*buffers[way][:2], field, way, SHARE[parity]).start()

        by_parity(run)

    def await_all(field, way):
        def run(parity):
            keep(*buffers[way][:2], field, way, SHARE[parity]).wait()
            for d in range(1, GRID):
                share = SHARE[(parity + d) % 2 if way else parity]
                arrival(*buffers[way], field, lax.rem(me + d, GRID), share).wait_recv()

        by_parity(run)

    def await_sent(field, way):
        def run(parity):
            for d in range(1, GRID):
                share = SHARE[parity if way else (parity + d) % 2]
                exchange(*buffers[way], field, lax.rem(me + d, GRID), share).wait_send()

        by_parity(run)

    def band_rows(band):
        return pl.ds(pl.multiple_of(band * (SLAB * ROWS), 8), SLAB * ROWS)

    travel = ((band_out, band_in), (theirs_out, theirs_in))
    planes = SLAB // len(COLUMNS)

    def piece_rows(band, index):
        return pl.ds(pl.multiple_of((band * SLAB + index * planes) * ROWS, 8), planes * ROWS)

    def stop_rows(way, band):
        return pl.ds((way * 2 + band) * planes * ROWS, planes * ROWS)

    def to_block(way, band):
        source, target = travel[way]
        return pltpu.make_async_remote_copy(
            src_ref=source.at[band_rows(band)],
            dst_ref=target.at[band_rows(band)],
            send_sem=blk_send.at[way, band],
            recv_sem=blk_recv.at[way, band],
            device_id=((after, before)[way], me),
            device_id_type=MESH,
        )

    def to_column(way, band, index):
        if COLUMNS[index] == BETWEEN[way]:
            target = travel[way][1].at[piece_rows(band, index)]
            done = last_recv.at[way, band, index]
            place = other_layer(way) + BETWEEN[1 - way]
        else:
            target, done = stop.at[stop_rows(way, band)], stop_recv.at[way, band]
            place = layer + COLUMNS[index]
        return pltpu.make_async_remote_copy(
            src_ref=travel[way][0].at[piece_rows(band, index)],
            dst_ref=target,
            send_sem=first_send.at[way, band, index],
            recv_sem=done,
            device_id=(place, me),
            device_id_type=MESH,
        )

    def from_column(way, band, index):
        return pltpu.make_async_remote_copy(
            src_ref=stop.at[stop_rows(way, band)],
            dst_ref=travel[way][1].at[piece_rows(band, index)],
            send_sem=second_send.at[way, band],
            recv_sem=last_recv.at[way, band, index],
            device_id=(other_layer(way) + BETWEEN[1 - way], me),
            device_id_type=MESH,
        )

    def depart(way, band):
        start = BETWEEN[way]

        @pl.when(column != start)
        def _():
            to_block(way, band).start()

        @pl.when(column == start)
        def _():
            for index in range(len(COLUMNS)):
                to_column(way, band, index).start()

    def relay_in(way, band):
        @pl.when(relays & (column != BETWEEN[way]))
        def _():
            to_column(way, band, COLUMNS.index(BETWEEN[1 - way])).wait_recv()
            from_column(way, band, piece).start()

    def arrive(way, band):
        end = BETWEEN[1 - way]

        @pl.when(column != end)
        def _():
            to_block(way, band).wait_recv()

        @pl.when(column == end)
        def _():
            for index in range(len(COLUMNS)):
                from_column(way, band, index).wait_recv()

    def departed(way, band):
        start = BETWEEN[way]

        @pl.when(column != start)
        def _():
            to_block(way, band).wait_send()

        @pl.when(column == start)
        def _():
            for index in range(len(COLUMNS)):
                to_column(way, band, index).wait_send()

        @pl.when(relays & (column != start))
        def _():
            from_column(way, band, 0).wait_send()

    def put_packed(ref, band, x, plane):
        start = pl.multiple_of((band * SLAB + x) * ROWS, 8)
        for k, part in enumerate(pack(plane)):
            ref[pl.ds(start + 24 * k, 24), :] = part

    def get_packed(ref, band, x):
        start = pl.multiple_of((band * SLAB + x) * ROWS, 8)
        return unpack([ref[pl.ds(start + 24 * k, 24), :] for k in range(3)])

    for band in range(2):

        @pl.loop(0, SLAB)
        def _(x):
            plane = own_ref[band, x]
            bands[band, x] = plane
            put_packed(band_out, band, x, plane)

        if band == 0:
            pl.semaphore_wait(barrier, peers)
        depart(0, band)

    acc[...] = jnp.zeros_like(acc)

    def pair(field):
        first = jnp.where(field < 3, field // 2, (field + 1) % 2)
        second = jnp.where(field < 3, (field + 1) // 2, 2 + (field - 3) // 2)
        return first, second

    def forward(field):
        first, second = pair(field)
        for group in range(0, SLAB, 4):
            density = bands[first, pl.ds(group, 4)] * bands[second, pl.ds(group, 4)]
            along_z = from_right(density.reshape(4 * NG, NG), right_ref)
            for i in range(4):
                plane = from_left(plane_ref[...], along_z[i * NG : (i + 1) * NG])
                parts = pack(plane)
                base = field * (GRID * MSG) + group + i
                for t in range(8):
                    tile = parts[t // 3][t % 3 * 8 : t % 3 * 8 + 8]
                    sent[pl.ds(base + t * SLAB, GRID, stride=MSG), :] = tile
                for t in (8, 9):
                    tile = parts[2][4 * t - 16 : 4 * t - 12]
                    sent[pl.ds(base + MSG + t * SLAB, GRID // 2, stride=2 * MSG), :] = tile

    def make_coulomb():
        factor = 4.0 * np.pi / (2.0 * np.pi / BOX_EDGE) ** 2 / float(NG) ** 3

        def square(index):
            folded = jnp.minimum(index, NG - index)
            return folded * folded

        kx = lax.broadcasted_iota(jnp.int32, (NG, 128), 0)
        lane = lax.broadcasted_iota(jnp.int32, (NG, 128), 1)

        @pl.loop(0, SHARE[1])
        def _(t):
            row = jnp.where(t < 8, t * GRID + me, 32 + 4 * t + me // 2)
            part, a = row // 24, row % 24
            ky = jnp.where(lane < NG, 24 * part + a, 72 + a)
            kz = jnp.where(lane < NG, lane, 32 * part + lane - NG)
            total = square(kx) + square(ky) + square(kz)
            safe = jnp.maximum(total, 1).astype(F32)
            coulomb[t] = jnp.where(total > 0, factor / safe, 0.0)

    def solve(field):
        await_all(field, 0)
        base = field * (GRID * MSG)

        def solve_tile(t):
            rows = jnp.concatenate(
                [got[pl.ds(base + t * SLAB + x, GRID, stride=MSG), :] for x in range(SLAB)],
                axis=0,
            )
            spectrum = from_left(there_ref[...], rows) * coulomb[t]
            mixed = from_left(back_ref[...], spectrum)
            for x in range(SLAB):
                ret_sent[pl.ds(base + t * SLAB + x, GRID, stride=MSG), :] = mixed[
                    x * GRID : (x + 1) * GRID
                ]

        for t in range(SHARE[0]):
            solve_tile(t)

        @pl.when(me % 2 == 1)
        def _():
            for t in range(SHARE[0], SHARE[1]):
                solve_tile(t)

        send_all(field, 1)

    def backward(field):
        await_all(field, 1)
        first, second = pair(field)
        base = field * (GRID * MSG)
        for group in range(0, SLAB, 4):
            planes = []
            for i in range(4):
                tiles = [
                    ret_got[pl.ds(base + t * SLAB + group + i, GRID, stride=MSG), :]
                    for t in range(8)
                ]
                start = base + MSG + group + i
                halves = [
                    ret_got[pl.ds(start + t * SLAB, GRID // 2, stride=2 * MSG), :]
                    for t in (8, 9)
                ]
                tiles.append(jnp.concatenate(halves, axis=0))
                parts = [jnp.concatenate(tiles[3 * k : 3 * k + 3], axis=0) for k in range(3)]
                planes.append(from_left(plane_ref[...], unpack(parts)))
            potential = from_right(jnp.concatenate(planes, axis=0), right_ref)
            potential = potential.reshape(4, NG, NG)
            here = pl.ds(group, 4)
            acc[first, here] += potential * bands[second, here]

            @pl.when(first != second)
            def _():
                acc[second, here] += potential * bands[first, here]

    def give_back(band):
        @pl.loop(0, SLAB)
        def _(x):
            put_packed(theirs_out, band, x, acc[2 + band, x])

        depart(1, band)

    def at(step, fields):
        return sum(jnp.where(step == i, field, 0) for i, field in enumerate(fields))

    @pl.loop(0, len(FORWARD))
    def _(step):
        for band in range(2):

            @pl.when(step == 3 + 2 * band)
            def _():
                arrive(0, band)

                @pl.loop(0, SLAB)
                def _(x):
                    bands[2 + band, x] = get_packed(band_in, band, x)

        forward_field = at(step, FORWARD)

        @pl.when(forward_field >= 0)
        def _():
            forward(forward_field)

        @pl.when(step == 1)
        def _():
            for band in range(2):
                relay_in(0, band)

        @pl.when(forward_field >= 0)
        def _():
            send_all(forward_field, 0)

        @pl.when(step == 2)
        def _():
            make_coulomb()

        solve_field = jnp.where(column == 0, at(step, SOLVE_FIRST), at(step, SOLVE))
        backward_field = at(step, BACKWARD)

        solve_late = (step == 10) | (step == 12) | ((step == 13) & (column != 0))

        @pl.when((solve_field >= 0) & ~solve_late)
        def _():
            solve(solve_field)

        @pl.when(backward_field >= 0)
        def _():
            backward(backward_field)

        @pl.when(step == 10)
        def _():
            give_back(0)

        @pl.when(step == 12)
        def _():
            give_back(1)

        @pl.when((solve_field >= 0) & solve_late)
        def _():
            solve(solve_field)

        for band in range(2):

            @pl.when(step == 12 + 2 * band)
            def _():
                relay_in(1, band)

    for band in range(2):
        arrive(1, band)

        @pl.loop(0, SLAB)
        def _(x):
            out_ref[band, x] = -(acc[band, x] + get_packed(theirs_in, band, x))

    @pl.loop(0, FIELDS)
    def _(field):
        for way in range(2):
            await_sent(field, way)

    for band in range(2):
        for way in range(2):
            departed(way, band)


def body(blocks, bands):
    count, slab, plane = bands.shape
    own = bands.reshape(count, slab, NG, NG)
    constants = [jnp.asarray(table) for table in tables()]
    vmem = pl.BlockSpec(memory_space=pltpu.VMEM)
    messages = pltpu.VMEM((FIELDS * GRID * MSG, 128), F32)
    packed = pltpu.VMEM((count * SLAB * ROWS, 128), F32)
    stops = pltpu.VMEM((2 * count * (SLAB // len(COLUMNS)) * ROWS, 128), F32)
    out = pl.pallas_call(
        functools.partial(kernel, blocks),
        out_shape=jax.ShapeDtypeStruct((count, slab, NG, NG), F32),
        in_specs=[vmem] * 5,
        out_specs=vmem,
        scratch_shapes=[
            pltpu.VMEM((2 * count, SLAB, NG, NG), F32),
            pltpu.VMEM((2 * count, SLAB, NG, NG), F32),
            pltpu.VMEM((SHARE[1], NG, 128), F32),
            messages,
            messages,
            messages,
            messages,
            packed,
            packed,
            packed,
            packed,
            pltpu.SemaphoreType.DMA((FIELDS, GRID)),
            pltpu.SemaphoreType.DMA((FIELDS, GRID)),
            pltpu.SemaphoreType.DMA((FIELDS, GRID)),
            pltpu.SemaphoreType.DMA((FIELDS, GRID)),
            pltpu.SemaphoreType.DMA((2, FIELDS)),
            pltpu.SemaphoreType.DMA((2, 2)),
            pltpu.SemaphoreType.DMA((2, 2)),
            stops,
            pltpu.SemaphoreType.DMA((2, 2, len(COLUMNS))),
            pltpu.SemaphoreType.DMA((2, 2)),
            pltpu.SemaphoreType.DMA((2, 2)),
            pltpu.SemaphoreType.DMA((2, 2, len(COLUMNS))),
        ],
        compiler_params=pltpu.CompilerParams(
            collective_id=0, has_side_effects=True, vmem_limit_bytes=48 * 1024 * 1024
        ),
    )(own, *constants)
    return out.reshape(count, slab, plane)


def solution(mesh):
    spec = P("blk", "grid", None)
    return jax.shard_map(
        functools.partial(body, mesh.shape["blk"]),
        mesh=mesh,
        in_specs=(spec,),
        out_specs=spec,
        check_vma=False,
    )
```

```python
import functools

import jax
import jax.numpy as jnp
import ml_dtypes
import numpy as np
from jax import lax
from jax.experimental import pallas as pl
from jax.experimental.pallas import tpu as pltpu
from jax.sharding import PartitionSpec as P

NG = 96
BOX_EDGE = 23.47
MESH = pl.DeviceIdType.MESH
F32 = jnp.float32
BF16 = jnp.bfloat16

GRID = 8
SLAB = NG // GRID
ROWS = NG * NG // 128
SHARE = 8, 10
MSG = SHARE[1] * SLAB
FIELDS = 7

LAYER = 16
COLUMNS = (0, 1, 2, 3, 4, 7, 8, 11, 12, 13, 14, 15, 5, 6, 9, 10)
LARGE = 12
PIECE = 56, 48
BETWEEN = LAYER - 1, 0

FORWARD = (0, 1, 2, 3, 4, 5, 6, -1, -1, -1, -1, -1, -1, -1, -1, -1)
SOLVE = (-1, -1, -1, -1, -1, -1, -1, 3, 4, 5, 6, 0, 1, 2, -1, -1)
BACKWARD = (-1, -1, -1, -1, -1, -1, -1, -1, -1, 3, 4, 5, 6, 0, 1, 2)


def hartley(rows, cols):
    angle = (rows[:, None] * cols[None, :] % NG) * (2.0 * np.pi / NG)
    return np.cos(angle) + np.sin(angle)


def split_table(table):
    parts = []
    for _ in range(3):
        part = table.astype(np.float32).astype(ml_dtypes.bfloat16)
        parts.append(part)
        table = table - part.astype(np.float64)
    return parts


def left_table(table):
    return np.concatenate([np.concatenate([part, part], axis=1) for part in split_table(table)])


def right_table(table):
    parts = [np.pad(part, ((0, 0), (0, 128 - NG))) for part in split_table(table)]
    return np.concatenate(parts, axis=1)


def tables():
    plain = np.arange(NG)
    mixed = np.arange(NG) % GRID * SLAB + np.arange(NG) // GRID
    return (
        right_table(hartley(plain, plain)),
        left_table(hartley(plain, plain)),
        left_table(hartley(plain, mixed)),
        left_table(hartley(mixed, plain)),
    )


def split(value):
    high = value.astype(BF16)
    low = (value - high.astype(F32)).astype(BF16)
    return high, low


def dot(a, b):
    return jnp.dot(a, b, preferred_element_type=F32)


def from_left(table, value):
    high, low = split(value)
    both = dot(table, jnp.concatenate([high, low], axis=0))
    return both[:NG] + (both[NG : 2 * NG] + both[2 * NG :])


def from_right(value, right_ref):
    high, low = split(value)
    above = dot(high, right_ref[:, :256])
    below = dot(low, right_ref[:, :256])
    rest = dot(high, right_ref[:, 256:])
    second = above[:, 128 : 128 + NG] + below[:, :NG]
    return above[:, :NG] + (second + (below[:, 128 : 128 + NG] + rest[:, :NG]))


def pack(plane):
    last = plane[72:96]
    return [
        jnp.concatenate([plane[24 * k : 24 * k + 24], last[:, 32 * k : 32 * k + 32]], axis=1)
        for k in range(3)
    ]


def unpack(parts):
    last = jnp.concatenate([part[:, 96:128] for part in parts], axis=1)
    return jnp.concatenate([part[:, :96] for part in parts] + [last], axis=0)


def kernel(
    blocks,
    own_ref,
    right_ref,
    plane_ref,
    there_ref,
    back_ref,
    out_ref,
    bands,
    acc,
    coulomb,
    sent,
    got,
    ret_sent,
    ret_got,
    band_out,
    band_in,
    theirs_out,
    theirs_in,
    fwd_send,
    fwd_recv,
    bwd_send,
    bwd_recv,
    self_sem,
    blk_send,
    blk_recv,
    stop,
    first_send,
    stop_recv,
    second_send,
    last_recv,
):
    blk = lax.axis_index("blk")
    me = lax.axis_index("grid")
    after = lax.rem(blk + 1, blocks)
    before = lax.rem(blk + blocks - 1, blocks)

    column = lax.rem(blk, LAYER)
    layer = blk - column
    piece = sum(jnp.where(column == c, i, 0) for i, c in enumerate(COLUMNS))
    relays = functools.reduce(jnp.logical_or, [column == c for c in COLUMNS])

    barrier = pltpu.get_barrier_semaphore()

    def greet(other):
        pl.semaphore_signal(barrier, inc=1, device_id=other, device_id_type=MESH)

    for d in range(1, GRID):
        greet((blk, lax.rem(me + d, GRID)))

    at_end = (column == 0) | (column == LAYER - 1)
    peers = GRID - 1 + jnp.where(relays, jnp.where(at_end, len(COLUMNS) + 1, 2), 0)
    for c in range(LAYER):
        linked = (column == c - 1) | (column == c + 1)
        if c in COLUMNS:
            linked = linked | ((relays if c in BETWEEN else at_end) & (column != c))
        peers = peers + jnp.where(linked, 1, 0)

        @pl.when(linked)
        def _():
            greet((layer + c, me))

    def other_layer(way):
        return lax.rem(layer + (LAYER if way == 0 else blocks - LAYER), blocks)

    for way, end in enumerate(BETWEEN):

        @pl.when(column == end)
        def _():
            for c in COLUMNS:
                greet((other_layer(way) + c, me))

        @pl.when(relays & (column != BETWEEN[1 - way]))
        def _():
            greet((other_layer(1 - way) + end, me))

    def message(field, device, share):
        return pl.ds(pl.multiple_of((field * GRID + device) * MSG, 8), share * SLAB)

    def exchange(source, target, send_sem, recv_sem, field, peer, share):
        return pltpu.make_async_remote_copy(
            src_ref=source.at[message(field, peer, share)],
            dst_ref=target.at[message(field, me, share)],
            send_sem=send_sem.at[field, peer],
            recv_sem=recv_sem.at[field, me],
            device_id=(blk, peer),
            device_id_type=MESH,
        )

    def arrival(source, target, send_sem, recv_sem, field, peer, share):
        return pltpu.make_async_remote_copy(
            src_ref=source.at[message(field, peer, share)],
            dst_ref=target.at[message(field, peer, share)],
            send_sem=send_sem.at[field, peer],
            recv_sem=recv_sem.at[field, peer],
            device_id=(blk, peer),
            device_id_type=MESH,
        )

    def keep(source, target, field, way, share):
        here = message(field, me, share)
        return pltpu.make_async_copy(source.at[here], target.at[here], self_sem.at[way, field])

    buffers = ((sent, got, fwd_send, fwd_recv), (ret_sent, ret_got, bwd_send, bwd_recv))

    def by_parity(run):
        for parity in range(2):

            @pl.when(me % 2 == parity)
            def _():
                run(parity)

    def send_all(field, way):
        def run(parity):
            for d in (4, 3, 5, 2, 6, 1, 7):
                share = SHARE[parity if way else (parity + d) % 2]
                exchange(*buffers[way], field, lax.rem(me + d, GRID), share).start()
            keep(*buffers[way][:2], field, way, SHARE[parity]).start()

        by_parity(run)

    def await_all(field, way):
        def run(parity):
            keep(*buffers[way][:2], field, way, SHARE[parity]).wait()
            for d in range(1, GRID):
                share = SHARE[(parity + d) % 2 if way else parity]
                arrival(*buffers[way], field, lax.rem(me + d, GRID), share).wait_recv()

        by_parity(run)

    def await_sent(field, way):
        def run(parity):
            for d in range(1, GRID):
                share = SHARE[parity if way else (parity + d) % 2]
                exchange(*buffers[way], field, lax.rem(me + d, GRID), share).wait_send()

        by_parity(run)

    def band_rows(band):
        return pl.ds(pl.multiple_of(band * (SLAB * ROWS), 8), SLAB * ROWS)

    travel = ((band_out, band_in), (theirs_out, theirs_in))

    def piece_rows(band, index, size):
        start = index * PIECE[0]
        if size == PIECE[1]:
            start = LARGE * PIECE[0] + (index - LARGE) * PIECE[1]
        return pl.ds(pl.multiple_of(band * (SLAB * ROWS) + start, 8), size)

    def stop_rows(way, band, size):
        return pl.ds((way * 2 + band) * PIECE[0], size)

    def size_of(index):
        return PIECE[0] if index < LARGE else PIECE[1]

    def to_block(way, band):
        source, target = travel[way]
        return pltpu.make_async_remote_copy(
            src_ref=source.at[band_rows(band)],
            dst_ref=target.at[band_rows(band)],
            send_sem=blk_send.at[way, band],
            recv_sem=blk_recv.at[way, band],
            device_id=((after, before)[way], me),
            device_id_type=MESH,
        )

    def to_column(way, band, index):
        if COLUMNS[index] == BETWEEN[way]:
            target = travel[way][1].at[piece_rows(band, index, size_of(index))]
            done = last_recv.at[way, band, index]
            place = other_layer(way) + BETWEEN[1 - way]
        else:
            target, done = stop.at[stop_rows(way, band, size_of(index))], stop_recv.at[way, band]
            place = layer + COLUMNS[index]
        return pltpu.make_async_remote_copy(
            src_ref=travel[way][0].at[piece_rows(band, index, size_of(index))],
            dst_ref=target,
            send_sem=first_send.at[way, band, index],
            recv_sem=done,
            device_id=(place, me),
            device_id_type=MESH,
        )

    def from_column(way, band, index, size):
        return pltpu.make_async_remote_copy(
            src_ref=stop.at[stop_rows(way, band, size)],
            dst_ref=travel[way][1].at[piece_rows(band, index, size)],
            send_sem=second_send.at[way, band],
            recv_sem=last_recv.at[way, band, index],
            device_id=(other_layer(way) + BETWEEN[1 - way], me),
            device_id_type=MESH,
        )

    def depart(way, band):
        start = BETWEEN[way]

        @pl.when(column != start)
        def _():
            to_block(way, band).start()

        @pl.when(column == start)
        def _():
            for index in range(len(COLUMNS)):
                to_column(way, band, index).start()

    def relay_in(way, band):
        @pl.when(relays & (column != BETWEEN[way]))
        def _():
            for index, large in ((COLUMNS.index(BETWEEN[1 - way]), True), (LARGE, False)):

                @pl.when((piece < LARGE) == large)
                def _():
                    to_column(way, band, index).wait_recv()
                    from_column(way, band, piece, size_of(index)).start()

    def arrive(way, band):
        end = BETWEEN[1 - way]

        @pl.when(column != end)
        def _():
            to_block(way, band).wait_recv()

        @pl.when(column == end)
        def _():
            for index in range(len(COLUMNS)):
                from_column(way, band, index, size_of(index)).wait_recv()

    def departed(way, band):
        start = BETWEEN[way]

        @pl.when(column != start)
        def _():
            to_block(way, band).wait_send()

        @pl.when(column == start)
        def _():
            for index in range(len(COLUMNS)):
                to_column(way, band, index).wait_send()

        @pl.when(relays & (column != start))
        def _():
            for size, large in zip(PIECE, (True, False)):

                @pl.when((piece < LARGE) == large)
                def _():
                    from_column(way, band, piece, size).wait_send()

    def put_packed(ref, band, x, plane):
        start = pl.multiple_of((band * SLAB + x) * ROWS, 8)
        for k, part in enumerate(pack(plane)):
            ref[pl.ds(start + 24 * k, 24), :] = part

    def get_packed(ref, band, x):
        start = pl.multiple_of((band * SLAB + x) * ROWS, 8)
        return unpack([ref[pl.ds(start + 24 * k, 24), :] for k in range(3)])

    for band in range(2):

        @pl.loop(0, SLAB)
        def _(x):
            plane = own_ref[band, x]
            bands[band, x] = plane
            put_packed(band_out, band, x, plane)

    pl.semaphore_wait(barrier, peers)
    for band in range(2):
        depart(0, band)

    acc[...] = jnp.zeros_like(acc)

    def pair(field):
        first = jnp.where(field < 3, field // 2, (field + 1) % 2)
        second = jnp.where(field < 3, (field + 1) // 2, 2 + (field - 3) // 2)
        return first, second

    def forward(field):
        first, second = pair(field)
        for group in range(0, SLAB, 4):
            density = bands[first, pl.ds(group, 4)] * bands[second, pl.ds(group, 4)]
            along_z = from_right(density.reshape(4 * NG, NG), right_ref)
            for i in range(4):
                plane = from_left(plane_ref[...], along_z[i * NG : (i + 1) * NG])
                parts = pack(plane)
                base = field * (GRID * MSG) + group + i
                for t in range(8):
                    tile = parts[t // 3][t % 3 * 8 : t % 3 * 8 + 8]
                    sent[pl.ds(base + t * SLAB, GRID, stride=MSG), :] = tile
                for t in (8, 9):
                    tile = parts[2][4 * t - 16 : 4 * t - 12]
                    sent[pl.ds(base + MSG + t * SLAB, GRID // 2, stride=2 * MSG), :] = tile

    def make_coulomb():
        factor = 4.0 * np.pi / (2.0 * np.pi / BOX_EDGE) ** 2 / float(NG) ** 3

        def square(index):
            folded = jnp.minimum(index, NG - index)
            return folded * folded

        kx = lax.broadcasted_iota(jnp.int32, (NG, 128), 0)
        lane = lax.broadcasted_iota(jnp.int32, (NG, 128), 1)

        @pl.loop(0, SHARE[1])
        def _(t):
            row = jnp.where(t < 8, t * GRID + me, 32 + 4 * t + me // 2)
            part, a = row // 24, row % 24
            ky = jnp.where(lane < NG, 24 * part + a, 72 + a)
            kz = jnp.where(lane < NG, lane, 32 * part + lane - NG)
            total = square(kx) + square(ky) + square(kz)
            safe = jnp.maximum(total, 1).astype(F32)
            coulomb[t] = jnp.where(total > 0, factor / safe, 0.0)

    def solve(field):
        await_all(field, 0)
        base = field * (GRID * MSG)

        def solve_tile(t):
            rows = jnp.concatenate(
                [got[pl.ds(base + t * SLAB + x, GRID, stride=MSG), :] for x in range(SLAB)],
                axis=0,
            )
            spectrum = from_left(there_ref[...], rows) * coulomb[t]
            mixed = from_left(back_ref[...], spectrum)
            for x in range(SLAB):
                ret_sent[pl.ds(base + t * SLAB + x, GRID, stride=MSG), :] = mixed[
                    x * GRID : (x + 1) * GRID
                ]

        for t in range(SHARE[0]):
            solve_tile(t)

        @pl.when(me % 2 == 1)
        def _():
            for t in range(SHARE[0], SHARE[1]):
                solve_tile(t)

        send_all(field, 1)

    def backward(field):
        await_all(field, 1)
        first, second = pair(field)
        base = field * (GRID * MSG)
        for group in range(0, SLAB, 4):
            planes = []
            for i in range(4):
                tiles = [
                    ret_got[pl.ds(base + t * SLAB + group + i, GRID, stride=MSG), :]
                    for t in range(8)
                ]
                start = base + MSG + group + i
                halves = [
                    ret_got[pl.ds(start + t * SLAB, GRID // 2, stride=2 * MSG), :]
                    for t in (8, 9)
                ]
                tiles.append(jnp.concatenate(halves, axis=0))
                parts = [jnp.concatenate(tiles[3 * k : 3 * k + 3], axis=0) for k in range(3)]
                planes.append(from_left(plane_ref[...], unpack(parts)))
            potential = from_right(jnp.concatenate(planes, axis=0), right_ref)
            potential = potential.reshape(4, NG, NG)
            here = pl.ds(group, 4)
            acc[first, here] += potential * bands[second, here]

            @pl.when(first != second)
            def _():
                acc[second, here] += potential * bands[first, here]

    def give_back(band):
        @pl.loop(0, SLAB)
        def _(x):
            put_packed(theirs_out, band, x, acc[2 + band, x])

        depart(1, band)

    def at(step, fields):
        return sum(jnp.where(step == i, field, 0) for i, field in enumerate(fields))

    @pl.loop(0, len(FORWARD))
    def _(step):
        @pl.when(step == 3)
        def _():
            for band in range(2):
                arrive(0, band)

                @pl.loop(0, SLAB)
                def _(x):
                    bands[2 + band, x] = get_packed(band_in, band, x)

        forward_field = at(step, FORWARD)

        @pl.when(forward_field >= 0)
        def _():
            forward(forward_field)

        @pl.when(step == 1)
        def _():
            for band in range(2):
                relay_in(0, band)

        @pl.when(forward_field >= 0)
        def _():
            send_all(forward_field, 0)

        @pl.when(step == 2)
        def _():
            make_coulomb()

        solve_field = at(step, SOLVE)
        backward_field = at(step, BACKWARD)

        @pl.when((solve_field >= 0) & (step < 12))
        def _():
            solve(solve_field)

        @pl.when(backward_field >= 0)
        def _():
            backward(backward_field)

        @pl.when(step == 10)
        def _():
            give_back(0)

        @pl.when(step == 12)
        def _():
            give_back(1)
            relay_in(1, 0)

        @pl.when(step == 13)
        def _():
            relay_in(1, 1)

        @pl.when((solve_field >= 0) & (step >= 12))
        def _():
            solve(solve_field)

    for band in range(2):
        arrive(1, band)

        @pl.loop(0, SLAB)
        def _(x):
            out_ref[band, x] = -(acc[band, x] + get_packed(theirs_in, band, x))

    @pl.loop(0, FIELDS)
    def _(field):
        for way in range(2):
            await_sent(field, way)

    for band in range(2):
        for way in range(2):
            departed(way, band)


def body(blocks, bands):
    count, slab, plane = bands.shape
    own = bands.reshape(count, slab, NG, NG)
    constants = [jnp.asarray(table) for table in tables()]
    vmem = pl.BlockSpec(memory_space=pltpu.VMEM)
    messages = pltpu.VMEM((FIELDS * GRID * MSG, 128), F32)
    packed = pltpu.VMEM((count * SLAB * ROWS, 128), F32)
    stops = pltpu.VMEM((2 * count * PIECE[0], 128), F32)
    out = pl.pallas_call(
        functools.partial(kernel, blocks),
        out_shape=jax.ShapeDtypeStruct((count, slab, NG, NG), F32),
        in_specs=[vmem] * 5,
        out_specs=vmem,
        scratch_shapes=[
            pltpu.VMEM((2 * count, SLAB, NG, NG), F32),
            pltpu.VMEM((2 * count, SLAB, NG, NG), F32),
            pltpu.VMEM((SHARE[1], NG, 128), F32),
            messages,
            messages,
            messages,
            messages,
            packed,
            packed,
            packed,
            packed,
            pltpu.SemaphoreType.DMA((FIELDS, GRID)),
            pltpu.SemaphoreType.DMA((FIELDS, GRID)),
            pltpu.SemaphoreType.DMA((FIELDS, GRID)),
            pltpu.SemaphoreType.DMA((FIELDS, GRID)),
            pltpu.SemaphoreType.DMA((2, FIELDS)),
            pltpu.SemaphoreType.DMA((2, 2)),
            pltpu.SemaphoreType.DMA((2, 2)),
            stops,
            pltpu.SemaphoreType.DMA((2, 2, len(COLUMNS))),
            pltpu.SemaphoreType.DMA((2, 2)),
            pltpu.SemaphoreType.DMA((2, 2)),
            pltpu.SemaphoreType.DMA((2, 2, len(COLUMNS))),
        ],
        compiler_params=pltpu.CompilerParams(
            collective_id=0, has_side_effects=True, vmem_limit_bytes=48 * 1024 * 1024
        ),
    )(own, *constants)
    return out.reshape(count, slab, plane)


def solution(mesh):
    spec = P("blk", "grid", None)
    return jax.shard_map(
        functools.partial(body, mesh.shape["blk"]),
        mesh=mesh,
        in_specs=(spec,),
        out_specs=spec,
        check_vma=False,
    )
```

```python
import functools

import jax
import jax.numpy as jnp
import ml_dtypes
import numpy as np
from jax import lax
from jax.experimental import pallas as pl
from jax.experimental.pallas import tpu as pltpu
from jax.sharding import PartitionSpec as P

NG = 96
BOX_EDGE = 23.47
MESH = pl.DeviceIdType.MESH
F32 = jnp.float32
BF16 = jnp.bfloat16

GRID = 8
SLAB = NG // GRID
ROWS = NG * NG // 128
SHARE = 8, 10
MSG = SHARE[1] * SLAB
FIELDS = 7

LAYER = 16
COLUMNS = (0, 1, 2, 3, 4, 7, 8, 11, 12, 13, 14, 15, 5, 6, 9, 10)
LARGE = 12
PIECE = 56, 48
BETWEEN = LAYER - 1, 0

FORWARD = (0, 1, 2, 3, 4, 5, 6, -1, -1, -1, -1, -1, -1, -1, -1, -1)
SOLVE = (-1, -1, -1, -1, -1, -1, -1, 3, 4, 5, 6, 0, 1, 2, -1, -1)
BACKWARD = (-1, -1, -1, -1, -1, -1, -1, -1, -1, 3, 4, 5, 6, 0, 1, 2)


def hartley(rows, cols):
    angle = (rows[:, None] * cols[None, :] % NG) * (2.0 * np.pi / NG)
    return np.cos(angle) + np.sin(angle)


def split_table(table):
    parts = []
    for _ in range(3):
        part = table.astype(np.float32).astype(ml_dtypes.bfloat16)
        parts.append(part)
        table = table - part.astype(np.float64)
    return parts


def left_table(table):
    return np.concatenate([np.concatenate([part, part], axis=1) for part in split_table(table)])


def right_table(table):
    parts = [np.pad(part, ((0, 0), (0, 128 - NG))) for part in split_table(table)]
    return np.concatenate(parts, axis=1)


def tables():
    plain = np.arange(NG)
    mixed = np.arange(NG) % GRID * SLAB + np.arange(NG) // GRID
    return (
        right_table(hartley(plain, plain)),
        left_table(hartley(plain, plain)),
        left_table(hartley(plain, mixed)),
        left_table(hartley(mixed, plain)),
    )


def split(value):
    high = value.astype(BF16)
    low = (value - high.astype(F32)).astype(BF16)
    return high, low


def dot(a, b):
    return jnp.dot(a, b, preferred_element_type=F32)


def from_left(table, value):
    high, low = split(value)
    both = dot(table, jnp.concatenate([high, low], axis=0))
    return both[:NG] + (both[NG : 2 * NG] + both[2 * NG :])


def from_right(value, right_ref):
    high, low = split(value)
    above = dot(high, right_ref[:, :256])
    below = dot(low, right_ref[:, :256])
    rest = dot(high, right_ref[:, 256:])
    second = above[:, 128 : 128 + NG] + below[:, :NG]
    return above[:, :NG] + (second + (below[:, 128 : 128 + NG] + rest[:, :NG]))


def pack(plane):
    last = plane[72:96]
    return [
        jnp.concatenate([plane[24 * k : 24 * k + 24], last[:, 32 * k : 32 * k + 32]], axis=1)
        for k in range(3)
    ]


def unpack(parts):
    last = jnp.concatenate([part[:, 96:128] for part in parts], axis=1)
    return jnp.concatenate([part[:, :96] for part in parts] + [last], axis=0)


def kernel(
    blocks,
    own_ref,
    right_ref,
    plane_ref,
    there_ref,
    back_ref,
    out_ref,
    bands,
    acc,
    coulomb,
    sent,
    got,
    ret_sent,
    ret_got,
    band_out,
    band_in,
    theirs_out,
    theirs_in,
    fwd_send,
    fwd_recv,
    bwd_send,
    bwd_recv,
    self_sem,
    blk_send,
    blk_recv,
    stop,
    first_send,
    stop_recv,
    second_send,
    last_recv,
):
    blk = lax.axis_index("blk")
    me = lax.axis_index("grid")
    after = lax.rem(blk + 1, blocks)
    before = lax.rem(blk + blocks - 1, blocks)

    column = lax.rem(blk, LAYER)
    layer = blk - column
    piece = sum(jnp.where(column == c, i, 0) for i, c in enumerate(COLUMNS))
    relays = functools.reduce(jnp.logical_or, [column == c for c in COLUMNS])

    barrier = pltpu.get_barrier_semaphore()

    def greet(other):
        pl.semaphore_signal(barrier, inc=1, device_id=other, device_id_type=MESH)

    for d in range(1, GRID):
        greet((blk, lax.rem(me + d, GRID)))

    at_end = (column == 0) | (column == LAYER - 1)
    peers = GRID - 1 + jnp.where(relays, jnp.where(at_end, len(COLUMNS) + 1, 2), 0)
    for c in range(LAYER):
        linked = (column == c - 1) | (column == c + 1)
        if c in COLUMNS:
            linked = linked | ((relays if c in BETWEEN else at_end) & (column != c))
        peers = peers + jnp.where(linked, 1, 0)

        @pl.when(linked)
        def _():
            greet((layer + c, me))

    def other_layer(way):
        return lax.rem(layer + (LAYER if way == 0 else blocks - LAYER), blocks)

    for way, end in enumerate(BETWEEN):

        @pl.when(column == end)
        def _():
            for c in COLUMNS:
                greet((other_layer(way) + c, me))

        @pl.when(relays & (column != BETWEEN[1 - way]))
        def _():
            greet((other_layer(1 - way) + end, me))

    def message(field, device, share):
        return pl.ds(pl.multiple_of((field * GRID + device) * MSG, 8), share * SLAB)

    def exchange(source, target, send_sem, recv_sem, field, peer, share):
        return pltpu.make_async_remote_copy(
            src_ref=source.at[message(field, peer, share)],
            dst_ref=target.at[message(field, me, share)],
            send_sem=send_sem.at[field, peer],
            recv_sem=recv_sem.at[field, me],
            device_id=(blk, peer),
            device_id_type=MESH,
        )

    def arrival(source, target, send_sem, recv_sem, field, peer, share):
        return pltpu.make_async_remote_copy(
            src_ref=source.at[message(field, peer, share)],
            dst_ref=target.at[message(field, peer, share)],
            send_sem=send_sem.at[field, peer],
            recv_sem=recv_sem.at[field, peer],
            device_id=(blk, peer),
            device_id_type=MESH,
        )

    def keep(source, target, field, way, share):
        here = message(field, me, share)
        return pltpu.make_async_copy(source.at[here], target.at[here], self_sem.at[way, field])

    buffers = ((sent, got, fwd_send, fwd_recv), (ret_sent, ret_got, bwd_send, bwd_recv))

    def by_parity(run):
        for parity in range(2):

            @pl.when(me % 2 == parity)
            def _():
                run(parity)

    def send_all(field, way):
        def run(parity):
            for d in (4, 3, 5, 2, 6, 1, 7):
                share = SHARE[parity if way else (parity + d) % 2]
                exchange(*buffers[way], field, lax.rem(me + d, GRID), share).start()
            keep(*buffers[way][:2], field, way, SHARE[parity]).start()

        by_parity(run)

    def await_all(field, way):
        def run(parity):
            keep(*buffers[way][:2], field, way, SHARE[parity]).wait()
            for d in range(1, GRID):
                share = SHARE[(parity + d) % 2 if way else parity]
                arrival(*buffers[way], field, lax.rem(me + d, GRID), share).wait_recv()

        by_parity(run)

    def await_sent(field, way):
        def run(parity):
            for d in range(1, GRID):
                share = SHARE[parity if way else (parity + d) % 2]
                exchange(*buffers[way], field, lax.rem(me + d, GRID), share).wait_send()

        by_parity(run)

    def band_rows(band):
        return pl.ds(pl.multiple_of(band * (SLAB * ROWS), 8), SLAB * ROWS)

    travel = ((band_out, band_in), (theirs_out, theirs_in))

    def piece_rows(band, index, size):
        start = index * PIECE[0]
        if size == PIECE[1]:
            start = LARGE * PIECE[0] + (index - LARGE) * PIECE[1]
        return pl.ds(pl.multiple_of(band * (SLAB * ROWS) + start, 8), size)

    def stop_rows(way, band, size):
        return pl.ds((way * 2 + band) * PIECE[0], size)

    def size_of(index):
        return PIECE[0] if index < LARGE else PIECE[1]

    def to_block(way, band):
        source, target = travel[way]
        return pltpu.make_async_remote_copy(
            src_ref=source.at[band_rows(band)],
            dst_ref=target.at[band_rows(band)],
            send_sem=blk_send.at[way, band],
            recv_sem=blk_recv.at[way, band],
            device_id=((after, before)[way], me),
            device_id_type=MESH,
        )

    def to_column(way, band, index):
        if COLUMNS[index] == BETWEEN[way]:
            target = travel[way][1].at[piece_rows(band, index, size_of(index))]
            done = last_recv.at[way, band, index]
            place = other_layer(way) + BETWEEN[1 - way]
        else:
            target, done = stop.at[stop_rows(way, band, size_of(index))], stop_recv.at[way, band]
            place = layer + COLUMNS[index]
        return pltpu.make_async_remote_copy(
            src_ref=travel[way][0].at[piece_rows(band, index, size_of(index))],
            dst_ref=target,
            send_sem=first_send.at[way, band, index],
            recv_sem=done,
            device_id=(place, me),
            device_id_type=MESH,
        )

    def from_column(way, band, index, size):
        return pltpu.make_async_remote_copy(
            src_ref=stop.at[stop_rows(way, band, size)],
            dst_ref=travel[way][1].at[piece_rows(band, index, size)],
            send_sem=second_send.at[way, band],
            recv_sem=last_recv.at[way, band, index],
            device_id=(other_layer(way) + BETWEEN[1 - way], me),
            device_id_type=MESH,
        )

    def depart(way, band):
        start = BETWEEN[way]

        @pl.when(column != start)
        def _():
            to_block(way, band).start()

        @pl.when(column == start)
        def _():
            for index in range(len(COLUMNS)):
                to_column(way, band, index).start()

    def relay_in(way, band):
        @pl.when(relays & (column != BETWEEN[way]))
        def _():
            for index, large in ((COLUMNS.index(BETWEEN[1 - way]), True), (LARGE, False)):

                @pl.when((piece < LARGE) == large)
                def _():
                    to_column(way, band, index).wait_recv()
                    from_column(way, band, piece, size_of(index)).start()

    def arrive(way, band):
        end = BETWEEN[1 - way]

        @pl.when(column != end)
        def _():
            to_block(way, band).wait_recv()

        @pl.when(column == end)
        def _():
            for index in range(len(COLUMNS)):
                from_column(way, band, index, size_of(index)).wait_recv()

    def departed(way, band):
        start = BETWEEN[way]

        @pl.when(column != start)
        def _():
            to_block(way, band).wait_send()

        @pl.when(column == start)
        def _():
            for index in range(len(COLUMNS)):
                to_column(way, band, index).wait_send()

        @pl.when(relays & (column != start))
        def _():
            for size, large in zip(PIECE, (True, False)):

                @pl.when((piece < LARGE) == large)
                def _():
                    from_column(way, band, piece, size).wait_send()

    def put_packed(ref, band, x, plane):
        start = pl.multiple_of((band * SLAB + x) * ROWS, 8)
        for k, part in enumerate(pack(plane)):
            ref[pl.ds(start + 24 * k, 24), :] = part

    def get_packed(ref, band, x):
        start = pl.multiple_of((band * SLAB + x) * ROWS, 8)
        return unpack([ref[pl.ds(start + 24 * k, 24), :] for k in range(3)])

    for band in range(2):

        @pl.loop(0, SLAB)
        def _(x):
            plane = own_ref[band, x]
            bands[band, x] = plane
            put_packed(band_out, band, x, plane)

    pl.semaphore_wait(barrier, peers)
    for band in range(2):
        depart(0, band)

    acc[...] = jnp.zeros_like(acc)

    def pair(field):
        first = jnp.where(field < 3, field // 2, (field + 1) % 2)
        second = jnp.where(field < 3, (field + 1) // 2, 2 + (field - 3) // 2)
        return first, second

    def forward(field):
        first, second = pair(field)
        for group in range(0, SLAB, 4):
            density = bands[first, pl.ds(group, 4)] * bands[second, pl.ds(group, 4)]
            along_z = from_right(density.reshape(4 * NG, NG), right_ref)
            for i in range(4):
                plane = from_left(plane_ref[...], along_z[i * NG : (i + 1) * NG])
                parts = pack(plane)
                base = field * (GRID * MSG) + group + i
                for t in range(8):
                    tile = parts[t // 3][t % 3 * 8 : t % 3 * 8 + 8]
                    sent[pl.ds(base + t * SLAB, GRID, stride=MSG), :] = tile
                for t in (8, 9):
                    tile = parts[2][4 * t - 16 : 4 * t - 12]
                    sent[pl.ds(base + MSG + t * SLAB, GRID // 2, stride=2 * MSG), :] = tile

    def make_coulomb():
        factor = 4.0 * np.pi / (2.0 * np.pi / BOX_EDGE) ** 2 / float(NG) ** 3

        def square(index):
            folded = jnp.minimum(index, NG - index)
            return folded * folded

        kx = lax.broadcasted_iota(jnp.int32, (NG, 128), 0)
        lane = lax.broadcasted_iota(jnp.int32, (NG, 128), 1)

        @pl.loop(0, SHARE[1])
        def _(t):
            row = jnp.where(t < 8, t * GRID + me, 32 + 4 * t + me // 2)
            part, a = row // 24, row % 24
            ky = jnp.where(lane < NG, 24 * part + a, 72 + a)
            kz = jnp.where(lane < NG, lane, 32 * part + lane - NG)
            total = square(kx) + square(ky) + square(kz)
            safe = jnp.maximum(total, 1).astype(F32)
            coulomb[t] = jnp.where(total > 0, factor / safe, 0.0)

    def solve(field):
        await_all(field, 0)
        base = field * (GRID * MSG)

        def solve_tile(t):
            rows = jnp.concatenate(
                [got[pl.ds(base + t * SLAB + x, GRID, stride=MSG), :] for x in range(SLAB)],
                axis=0,
            )
            spectrum = from_left(there_ref[...], rows) * coulomb[t]
            mixed = from_left(back_ref[...], spectrum)
            for x in range(SLAB):
                ret_sent[pl.ds(base + t * SLAB + x, GRID, stride=MSG), :] = mixed[
                    x * GRID : (x + 1) * GRID
                ]

        for t in range(SHARE[0]):
            solve_tile(t)

        @pl.when(me % 2 == 1)
        def _():
            for t in range(SHARE[0], SHARE[1]):
                solve_tile(t)

        send_all(field, 1)

    def backward(field):
        await_all(field, 1)
        first, second = pair(field)
        base = field * (GRID * MSG)
        for group in range(0, SLAB, 4):
            planes = []
            for i in range(4):
                tiles = [
                    ret_got[pl.ds(base + t * SLAB + group + i, GRID, stride=MSG), :]
                    for t in range(8)
                ]
                start = base + MSG + group + i
                halves = [
                    ret_got[pl.ds(start + t * SLAB, GRID // 2, stride=2 * MSG), :]
                    for t in (8, 9)
                ]
                tiles.append(jnp.concatenate(halves, axis=0))
                parts = [jnp.concatenate(tiles[3 * k : 3 * k + 3], axis=0) for k in range(3)]
                planes.append(from_left(plane_ref[...], unpack(parts)))
            potential = from_right(jnp.concatenate(planes, axis=0), right_ref)
            potential = potential.reshape(4, NG, NG)
            here = pl.ds(group, 4)
            acc[first, here] += potential * bands[second, here]

            @pl.when(first != second)
            def _():
                acc[second, here] += potential * bands[first, here]

    def give_back(band):
        @pl.loop(0, SLAB)
        def _(x):
            put_packed(theirs_out, band, x, acc[2 + band, x])

        depart(1, band)

    def at(step, fields):
        return sum(jnp.where(step == i, field, 0) for i, field in enumerate(fields))

    @pl.loop(0, len(FORWARD))
    def _(step):
        for band in range(2):

            @pl.when(step == 3 + 2 * band)
            def _():
                arrive(0, band)

                @pl.loop(0, SLAB)
                def _(x):
                    bands[2 + band, x] = get_packed(band_in, band, x)

        forward_field = at(step, FORWARD)

        @pl.when(forward_field >= 0)
        def _():
            forward(forward_field)

        @pl.when(step == 1)
        def _():
            for band in range(2):
                relay_in(0, band)

        @pl.when(forward_field >= 0)
        def _():
            send_all(forward_field, 0)

        @pl.when(step == 2)
        def _():
            make_coulomb()

        solve_field = at(step, SOLVE)
        backward_field = at(step, BACKWARD)

        @pl.when((solve_field >= 0) & (step < 12))
        def _():
            solve(solve_field)

        @pl.when(backward_field >= 0)
        def _():
            backward(backward_field)

        @pl.when(step == 10)
        def _():
            give_back(0)

        @pl.when(step == 12)
        def _():
            give_back(1)
            relay_in(1, 0)

        @pl.when((solve_field >= 0) & (step >= 12))
        def _():
            solve(solve_field)

        @pl.when(step == 13)
        def _():
            relay_in(1, 1)

    for band in range(2):
        arrive(1, band)

        @pl.loop(0, SLAB)
        def _(x):
            out_ref[band, x] = -(acc[band, x] + get_packed(theirs_in, band, x))

    @pl.loop(0, FIELDS)
    def _(field):
        for way in range(2):
            await_sent(field, way)

    for band in range(2):
        for way in range(2):
            departed(way, band)


def body(blocks, bands):
    count, slab, plane = bands.shape
    own = bands.reshape(count, slab, NG, NG)
    constants = [jnp.asarray(table) for table in tables()]
    vmem = pl.BlockSpec(memory_space=pltpu.VMEM)
    messages = pltpu.VMEM((FIELDS * GRID * MSG, 128), F32)
    packed = pltpu.VMEM((count * SLAB * ROWS, 128), F32)
    stops = pltpu.VMEM((2 * count * PIECE[0], 128), F32)
    out = pl.pallas_call(
        functools.partial(kernel, blocks),
        out_shape=jax.ShapeDtypeStruct((count, slab, NG, NG), F32),
        in_specs=[vmem] * 5,
        out_specs=vmem,
        scratch_shapes=[
            pltpu.VMEM((2 * count, SLAB, NG, NG), F32),
            pltpu.VMEM((2 * count, SLAB, NG, NG), F32),
            pltpu.VMEM((SHARE[1], NG, 128), F32),
            messages,
            messages,
            messages,
            messages,
            packed,
            packed,
            packed,
            packed,
            pltpu.SemaphoreType.DMA((FIELDS, GRID)),
            pltpu.SemaphoreType.DMA((FIELDS, GRID)),
            pltpu.SemaphoreType.DMA((FIELDS, GRID)),
            pltpu.SemaphoreType.DMA((FIELDS, GRID)),
            pltpu.SemaphoreType.DMA((2, FIELDS)),
            pltpu.SemaphoreType.DMA((2, 2)),
            pltpu.SemaphoreType.DMA((2, 2)),
            stops,
            pltpu.SemaphoreType.DMA((2, 2, len(COLUMNS))),
            pltpu.SemaphoreType.DMA((2, 2)),
            pltpu.SemaphoreType.DMA((2, 2)),
            pltpu.SemaphoreType.DMA((2, 2, len(COLUMNS))),
        ],
        compiler_params=pltpu.CompilerParams(
            collective_id=0, has_side_effects=True, vmem_limit_bytes=48 * 1024 * 1024
        ),
    )(own, *constants)
    return out.reshape(count, slab, plane)


def solution(mesh):
    spec = P("blk", "grid", None)
    return jax.shard_map(
        functools.partial(body, mesh.shape["blk"]),
        mesh=mesh,
        in_specs=(spec,),
        out_specs=spec,
        check_vma=False,
    )
```
